32 devices in a mesh: row: 4 (over y, x), grp: 8 (over z, core).
Axes of the slice: x: 2, y: 2, z: 4, core: 2. Of those that a mesh axis runs over, the one named last changes fastest.
Arguments:
- segments: bfloat16 [8, 64, 128, 512], P('grp', 'row'), may hold values from -40 to 40
- conv_weight: bfloat16 [3, 512, 512], replicated, may hold values from -0.15625 to 0.15625
- gain: float32 [512], replicated, may hold values from 0.1 to 1.9
- head: bfloat16 [512, 128], replicated, may hold values from -0.25 to 0.25
- group: int32 [8, 64], P('grp', 'row'), may hold values from 0 to 7
- positive: int32 [8, 64], P('grp', 'row'), may hold values from 0 to 63, as said below
Outputs:
- grad_conv: float32 [3, 512, 512], replicated
- grad_gain: float32 [512], replicated
- projector_derivative: float32 [512, 128], replicated
The draws below stay inside these ranges and needn't reach their ends.
Inputs may be any that keep to these rules, and one draw needn't show every extreme that they name: positive[c, i] is another segment of the same index c with the same group, and positive[c, positive[c, i]] == i.
All inputs are finite; a program needn't handle non-finite values.
Results may differ from the reference program's by a relative error of at most 0.003.
The reference program's roundings to bfloat16 on the way count: a program that leaves them out, or rounds other values in their place, can miss the bound.
Values sent between devices are 32-bit elements; how exact they have to be, the bound alone decides.
A program may use at most 64 MiB of HBM per device.

```python
import math
from functools import partial
import jax
import jax.numpy as jnp
from jax import lax

C = 512
PROJ = 128
LEN = 128
KERNEL = 3
DILATION_GAP = 2
GROUPS = 8
ROWSEGS = 64
COLS = 8


def pair_layout(key):
    column_keys = jax.random.split(jax.random.fold_in(key, 101), COLS)
    orders = jax.vmap(lambda one_key: jax.random.permutation(one_key, ROWSEGS))(column_keys).astype(jnp.int32)
    slot_index = jnp.arange(ROWSEGS, dtype=jnp.int32)
    partner_slot = jnp.bitwise_xor(slot_index, 1)
    draw_one = jax.random.randint(jax.random.fold_in(key, 202), (COLS, ROWSEGS // 2), 0, GROUPS, dtype=jnp.int32)
    draw_two = jax.random.randint(jax.random.fold_in(key, 303), (COLS, ROWSEGS // 2), 0, GROUPS, dtype=jnp.int32)
    pair_group = jnp.minimum(draw_one, draw_two).at[:, 0].set(GROUPS - 1).at[:, 1].set(0)
    slot_group = jnp.repeat(pair_group, 2, axis=1)
    column_rows = jnp.arange(COLS, dtype=jnp.int32)[:, None]
    partner_ids = jnp.zeros((COLS, ROWSEGS), jnp.int32).at[column_rows, orders].set(orders[:, partner_slot])
    group_ids = jnp.zeros((COLS, ROWSEGS), jnp.int32).at[column_rows, orders].set(slot_group)
    return (group_ids, partner_ids)


def draw_group(key, part):
    return pair_layout(key)[0]


def draw_positive(key, part):
    return pair_layout(key)[1]


def draw_segments(key, part):
    shape = (COLS, ROWSEGS, LEN, C)
    row_scale = jnp.exp(jax.random.uniform(jax.random.fold_in(key, 11), (COLS, ROWSEGS, LEN, 1), jnp.float32, 0.0, math.log(10.0)))
    chan_scale = jnp.exp(jax.random.uniform(jax.random.fold_in(key, 12), (1, 1, 1, C), jnp.float32, 0.0, math.log(10.0)))
    base = jax.random.truncated_normal(jax.random.fold_in(key, 15), -4.0, 4.0, shape, jnp.float32)
    return (base * row_scale * chan_scale * 0.1).astype(jnp.bfloat16)


def gaussian(key, extent, width, most, held_as=jnp.bfloat16):
    return jnp.clip(width * jax.random.normal(key, extent, jnp.float32), -most, most).astype(held_as)


def setup_inputs(seed: int = 0) -> dict:
    key_list = jax.random.split(jax.random.key(seed), 7)
    return {
        "segments": draw_segments(jax.random.fold_in(key_list[6], 71), 0),
        "conv_weight": gaussian(key_list[1], (KERNEL, C, C), (KERNEL * C) ** -0.5, 0.15625),
        "gain": jnp.clip(1.0 + 0.18 * jax.random.normal(key_list[2], (C,), jnp.float32), 0.1, 1.9),
        "head": gaussian(key_list[3], (C, PROJ), C ** -0.5, 0.25),
        "group": draw_group(jax.random.fold_in(key_list[6], 71), 0),
        "positive": draw_positive(jax.random.fold_in(key_list[6], 71), 0),
    }


logit_divisor = 0.1

def unit_rows(values):
    return values * lax.rsqrt(lax.optimization_barrier(jnp.mean(values * values, axis=-1, keepdims=True)) + 1e-05)

def scale_embed(projected):
    return unit_rows(projected) * projected.shape[-1] ** (-0.5)

def filter_tap_window(normalized_rows, filter_tap_index, spacing):
    sequence_length = normalized_rows.shape[1]
    padded = jnp.pad(normalized_rows, ((0, 0), (spacing, spacing), (0, 0)))
    return padded[:, filter_tap_index * spacing:filter_tap_index * spacing + sequence_length]

def reverse_tap_gather(term, filter_tap_index, spacing):
    sequence_length = term.shape[1]
    padded = jnp.pad(term, ((0, 0), (spacing, spacing), (0, 0)))
    begin = (2 - filter_tap_index) * spacing
    return padded[:, begin:begin + sequence_length]

def encode(patient_piece_records, conv_weight, gain, head):
    inputs = patient_piece_records.astype(jnp.float32)
    unit = unit_rows(inputs)
    normalized_rows = (unit * gain).astype(jnp.bfloat16)
    segment_count, sequence_length, channel_count = normalized_rows.shape
    conv = jnp.zeros((segment_count * sequence_length, channel_count), jnp.float32)
    for filter_tap_index in range(conv_weight.shape[0]):
        shifted_input = filter_tap_window(normalized_rows, filter_tap_index, DILATION_GAP).reshape(segment_count * sequence_length, channel_count)
        conv = conv + jnp.dot(shifted_input, conv_weight[filter_tap_index], preferred_element_type=jnp.float32)
    conv = conv.reshape(segment_count, sequence_length, channel_count)
    hidden = inputs + jax.nn.gelu(conv, approximate=True)
    pooled = lax.optimization_barrier(jnp.mean(hidden, axis=1)).astype(jnp.bfloat16)
    projected = jnp.dot(pooled, head, preferred_element_type=jnp.float32)
    return (unit, normalized_rows, conv, pooled, projected)

def backward(embed_grad, unit, normalized_rows, conv, pooled, projected, conv_weight, head):
    projected_grad = jax.vjp(scale_embed, projected)[1](embed_grad)[0]
    projector_derivative = jnp.dot(pooled.astype(jnp.float32).T, projected_grad, precision=lax.Precision.HIGHEST)
    pooled_grad = jnp.dot(projected_grad, head.astype(jnp.float32).T, precision=lax.Precision.HIGHEST)
    segment_count, sequence_length, channel_count = conv.shape
    hidden_grad = jnp.broadcast_to(pooled_grad[:, None, :] / sequence_length, conv.shape)
    conv_grad = jax.vjp(partial(jax.nn.gelu, approximate=True), conv)[1](hidden_grad)[0].astype(jnp.bfloat16)
    flat_grad = conv_grad.reshape(segment_count * sequence_length, channel_count)
    tap_grads = []
    normalized_gradient = jnp.zeros((segment_count, sequence_length, channel_count), jnp.float32)
    for filter_tap_index in range(conv_weight.shape[0]):
        shifted_input = filter_tap_window(normalized_rows, filter_tap_index, DILATION_GAP).reshape(segment_count * sequence_length, channel_count)
        tap_grads.append(lax.dot_general(shifted_input, flat_grad, (((0,), (0,)), ((), ())), preferred_element_type=jnp.float32))
        backward_term = lax.dot_general(flat_grad, conv_weight[filter_tap_index], (((1,), (1,)), ((), ())), preferred_element_type=jnp.float32)
        normalized_gradient = normalized_gradient + reverse_tap_gather(backward_term.reshape(segment_count, sequence_length, channel_count), filter_tap_index, DILATION_GAP)
    grad_conv = jnp.stack(tap_grads)
    grad_gain = lax.optimization_barrier(jnp.sum(normalized_gradient * unit, axis=(0, 1)))
    return (grad_conv, grad_gain, projector_derivative)

def reference(segments, conv_weight, gain, head, group, positive):
    matrix_width_number, matrix_height_number = group.shape
    global_multiplier = (matrix_width_number * matrix_height_number) ** (-0.5) / logit_divisor

    def embed_column(column_data):
        return scale_embed(encode(column_data, conv_weight, gain, head)[4])
    embeddings = lax.map(embed_column, segments)

    def column_grad(packed):
        encounter_latent_vector, group_ids, partners = packed
        cosine_affinity_matrix = jnp.dot(encounter_latent_vector, encounter_latent_vector.T, precision=lax.Precision.HIGHEST) / logit_divisor
        positions = jnp.arange(matrix_height_number, dtype=jnp.int32)
        same_group = (group_ids[:, None] == group_ids[None, :]) & (positions[:, None] != positions[None, :])
        log_total = jnp.log(lax.optimization_barrier(jnp.sum(jnp.where(same_group, jnp.exp(cosine_affinity_matrix), 0.0), axis=1)))
        softmax = jnp.where(same_group, jnp.exp(cosine_affinity_matrix - log_total[:, None]), 0.0)
        row_term = jnp.dot(softmax, encounter_latent_vector, precision=lax.Precision.HIGHEST)
        column_term = jnp.dot(softmax.T, encounter_latent_vector, precision=lax.Precision.HIGHEST)
        return global_multiplier * (row_term + column_term - 2.0 * encounter_latent_vector[partners])
    embed_grads = lax.map(column_grad, (embeddings, group, positive))

    def accumulate(carry, packed):
        column_data, embed_grad = packed
        unit, normalized_rows, conv, pooled, projected = encode(column_data, conv_weight, gain, head)
        terms = backward(embed_grad, unit, normalized_rows, conv, pooled, projected, conv_weight, head)
        return ((carry[0] + terms[0], carry[1] + terms[1], carry[2] + terms[2]), None)
    start_value = (jnp.zeros(conv_weight.shape, jnp.float32), jnp.zeros(gain.shape, jnp.float32), jnp.zeros(head.shape, jnp.float32))
    totals, _ = lax.scan(accumulate, start_value, (segments, embed_grads))
    return (totals[0], totals[1], totals[2])
```

```python
import functools
import math

import jax
import jax.numpy as jnp
from jax import lax
from jax.experimental import pallas as pl
from jax.experimental.pallas import tpu as pltpu
from jax.sharding import PartitionSpec as P

DILATION_GAP = 2
LOGIT_DIVISOR = 0.1
EPS = 1e-05
GELU_A = math.sqrt(2.0 / math.pi)
GELU_B = 0.044715
HIGHEST = lax.Precision.HIGHEST
MESH = pl.DeviceIdType.MESH
F32 = jnp.float32
BF16 = jnp.bfloat16
BLOCK_SEGS = 4


class Links:
    def __init__(self, send_sem, recv_sem):
        self.send_sem, self.recv_sem, self.count, self.copies = send_sem, recv_sem, 0, []

    def send(self, src, dst, device):
        copy = pltpu.make_async_remote_copy(
            src_ref=src,
            dst_ref=dst,
            send_sem=self.send_sem.at[self.count],
            recv_sem=self.recv_sem.at[self.count],
            device_id=device,
            device_id_type=MESH,
        )
        copy.start()
        self.count += 1
        self.copies.append(copy)
        return copy


def shift_rows(values, by, length):
    rows = values.shape[0]
    time = lax.rem(lax.broadcasted_iota(jnp.int32, values.shape, 0), length)
    keep = (time >= by) if by > 0 else (time < length + by)
    return jnp.where(keep, pltpu.roll(values, by % rows, 0), 0.0)


def kernel(
    dims,
    seg_ref,
    w_ref,
    gain_ref,
    head_ref,
    hot_ref,
    pos_ref,
    taps_out,
    proj_out,
    gain_out,
    x3,
    conv,
    n_t,
    unit,
    dgelu,
    pooled,
    hgrad,
    g3,
    embeds,
    acc,
    work,
    r_a1,
    r_b1,
    r_a2,
    r_b2,
    r_z,
    pacc,
    pwork,
    pr_a1,
    pr_b1,
    pr_a2,
    pr_b2,
    pr_z,
    gc,
    gl,
    gh,
    gz,
    send_sem,
    recv_sem,
):
    n_row, n_grp, n_hi, n_lo, n_z, total_segments = dims
    segs, length, chans = seg_ref.shape
    proj = head_ref.shape[1]
    n_taps = w_ref.shape[0]
    half = chans // 2
    quarter = chans // 4
    row = lax.axis_index("row")
    grp = lax.axis_index("grp")
    hi, lo = lax.div(row, n_lo), lax.rem(row, n_lo)
    z, core = lax.div(grp, 2), lax.rem(grp, 2)
    links = Links(send_sem, recv_sem)

    sibling = (row, z * 2 + (1 - core))
    row_peers = [(lax.rem(row + j, n_row), grp) for j in range(1, n_row)]
    lo_peers = [(lax.rem(lo + j, n_lo)) for j in range(1, n_lo)]
    hi_peers = [(lax.rem(hi + j, n_hi)) for j in range(1, n_hi)]
    z_peers = [(lax.rem(z + j, n_z)) for j in range(1, n_z)]

    def lo_dev(p):
        return (hi * n_lo + p, grp)

    def hi_dev(p):
        return (p * n_lo + lo, grp)

    def z_dev(p):
        return (row, p * 2 + core)

    barrier = pltpu.get_barrier_semaphore()
    everyone = [sibling] + row_peers + [z_dev(p) for p in z_peers]
    for device in everyone:
        pl.semaphore_signal(barrier, inc=1, device_id=device, device_id_type=MESH)

    block = BLOCK_SEGS * length

    @pl.loop(0, segs // BLOCK_SEGS)
    def _(b):
        @pl.loop(0, BLOCK_SEGS)
        def _(i):
            s = b * BLOCK_SEGS + i
            inputs = seg_ref[s].astype(F32)
            scale = lax.rsqrt(jnp.mean(inputs * inputs, axis=-1, keepdims=True) + EPS)
            normal = inputs * scale
            unit[s] = normal
            normed = normal * gain_ref[...]
            rows = pl.ds(pl.multiple_of(i * length, length), length)
            x3[rows, 0:chans] = shift_rows(normed, DILATION_GAP, length).astype(BF16)
            x3[rows, chans : 2 * chans] = normed.astype(BF16)
            x3[rows, 2 * chans : 3 * chans] = shift_rows(normed, -DILATION_GAP, length).astype(BF16)
            n_t[s] = normed.T.astype(BF16)

        conv[...] = jnp.dot(
            x3[...], w_ref[...].reshape(n_taps * chans, chans), preferred_element_type=F32
        )

        @pl.loop(0, BLOCK_SEGS)
        def _(i):
            s = b * BLOCK_SEGS + i
            total = jnp.zeros((8, chans), F32)
            step = 32
            for q in range(length // step):
                rows = pl.ds(pl.multiple_of(i * length + q * step, step), step)
                v = conv[rows, :]
                v2 = v * v
                th = jnp.tanh(GELU_A * (v + GELU_B * (v2 * v)))
                cdf = 0.5 * (1.0 + th)
                hidden = seg_ref[s, q * step : (q + 1) * step].astype(F32) + v * cdf
                dgelu[s, q * step : (q + 1) * step] = cdf + (0.5 * GELU_A) * v * (
                    1.0 - th * th
                ) * (1.0 + (3.0 * GELU_B) * v2)
                total = total + hidden.reshape(step // 8, 8, chans).sum(axis=0)
            pooled[pl.ds(s, 1), :] = jnp.sum(total, axis=0, keepdims=True) * (1.0 / length)

    pool16 = pooled[...].astype(BF16)
    projected = jnp.dot(pool16, head_ref[...], preferred_element_type=F32)
    inv = lax.rsqrt(jnp.mean(projected * projected, axis=-1, keepdims=True) + EPS)
    embed = projected * inv * proj ** (-0.5)
    embeds[row, :, 0:proj] = embed
    embeds[row, :, proj:] = hot_ref[...]
    pl.semaphore_wait(barrier, len(everyone))
    moves = [links.send(embeds.at[row], embeds.at[row], device) for device in row_peers]
    for move in moves:
        move.wait_recv()
    every = embeds[...].reshape(n_row * segs, 2 * proj)
    e_all, hot_all = every[:, :proj], every[:, proj:]
    count = n_row * segs
    contract = (((1,), (1,)), ((), ()))

    def scores_of(left):
        return (
            lax.dot_general(left, e_all, contract, precision=HIGHEST, preferred_element_type=F32)
            / LOGIT_DIVISOR
        )

    def same_of(left, first):
        match = lax.dot_general(left, hot_all, contract, preferred_element_type=F32)
        shape = match.shape
        own = first + lax.broadcasted_iota(jnp.int32, shape, 0)
        return jnp.where(own != lax.broadcasted_iota(jnp.int32, shape, 1), match, 0.0)

    s_full, m_full = scores_of(e_all), same_of(hot_all, 0)
    log_row = jnp.log(
        jnp.sum(jnp.where(m_full > 0.5, jnp.exp(s_full), 0.0), axis=0, keepdims=True)
    )
    s_own, m_own = scores_of(embed), same_of(hot_ref[...], row * segs) > 0.5
    log_own = jnp.log(jnp.sum(jnp.where(m_own, jnp.exp(s_own), 0.0), axis=1, keepdims=True))
    mix = jnp.where(m_own, jnp.exp(s_own - log_own) + jnp.exp(s_own - log_row), 0.0)
    mix = mix - jnp.where(
        pos_ref[...] == lax.broadcasted_iota(jnp.int32, (segs, count), 1), 2.0, 0.0
    )
    embed_grad = (total_segments ** (-0.5) / LOGIT_DIVISOR) * jnp.dot(
        mix, e_all, precision=HIGHEST, preferred_element_type=F32
    )
    inner = jnp.mean(embed_grad * projected, axis=-1, keepdims=True)
    projected_grad = proj ** (-0.5) * (embed_grad * inv - projected * (inv * inv * inv * inner))
    hgrad[...] = (
        lax.dot_general(
            projected_grad,
            head_ref[...].astype(F32),
            contract,
            precision=HIGHEST,
            preferred_element_type=F32,
        )
        / length
    )

    @pl.loop(0, segs)
    def _(s):
        grad = (dgelu[s] * hgrad[pl.ds(s, 1), :]).astype(BF16)
        grad32 = grad.astype(F32)
        rows = pl.ds(pl.multiple_of(s * length, length), length)
        shifted = (
            shift_rows(grad32, -DILATION_GAP, length).astype(BF16),
            grad,
            shift_rows(grad32, DILATION_GAP, length).astype(BF16),
        )
        for k in range(n_taps):
            g3[k, 0, rows, :] = shifted[k][:, :half]
            g3[k, 1, rows, :] = shifted[k][:, half:]

    def tiles(values, like):
        need = math.prod(like[:-1])
        if need > values.shape[0]:
            pad = jnp.zeros((need - values.shape[0], values.shape[1]), F32)
            values = jnp.concatenate([values, pad], axis=0)
        return values.reshape(like)

    def own_half(part):
        return pl.ds(pl.multiple_of(core * half, half), half) if part is None else pl.ds(
            pl.multiple_of(core * half + part * quarter, quarter), quarter
        )

    a_cols, b_cols = pl.ds(0, quarter), pl.ds(quarter, quarter)
    every_ = slice(None)

    class Chunk:
        def __init__(self, fill, acc_, work_, ra1, rb1, ra2, rb2, rz, out):
            self.fill, self.acc, self.w, self.out = fill, acc_, work_, out
            self.ra1, self.rb1, self.ra2, self.rb2, self.rz = ra1, rb1, ra2, rb2, rz
            self.moves = []

        def arrive(self):
            for move in self.moves:
                move.wait_recv()
            self.moves = []

        def go(self, src, dst, device):
            self.moves.append(links.send(src, dst, device))

        def stage0(self):
            self.fill(self.acc, 1 - core)
            self.go(self.acc.at[1 - core], self.w, sibling)
            self.fill(self.acc, core)

        def stage1(self):
            self.arrive()
            w = self.w
            w[...] = w[...] + self.acc[core]
            for j, p in enumerate(lo_peers):
                self.go(w.at[:, p, :, :, :, a_cols], self.ra1.at[j], lo_dev(p))
            for j, p in enumerate(hi_peers):
                self.go(w.at[p, :, :, :, :, b_cols], self.rb1.at[j], hi_dev(p))

        def stage2(self):
            self.arrive()
            w = self.w
            a = w[:, lo, :, :, :, a_cols]
            for j in range(n_lo - 1):
                a = a + self.ra1[j]
            w[:, lo, :, :, :, a_cols] = a
            b = w[hi, :, :, :, :, b_cols]
            for j in range(n_hi - 1):
                b = b + self.rb1[j]
            w[hi, :, :, :, :, b_cols] = b
            for j, p in enumerate(hi_peers):
                self.go(w.at[p, lo, :, :, :, a_cols], self.ra2.at[j], hi_dev(p))
            for j, p in enumerate(lo_peers):
                self.go(w.at[hi, p, :, :, :, b_cols], self.rb2.at[j], lo_dev(p))

        def stage3(self):
            self.arrive()
            w = self.w
            a = w[hi, lo, :, :, :, a_cols]
            for j in range(n_hi - 1):
                a = a + self.ra2[j]
            w[hi, lo, :, :, :, a_cols] = a
            b = w[hi, lo, :, :, :, b_cols]
            for j in range(n_lo - 1):
                b = b + self.rb2[j]
            w[hi, lo, :, :, :, b_cols] = b
            for j, p in enumerate(z_peers):
                self.go(w.at[hi, lo, p], self.rz.at[j], z_dev(p))

        def stage4(self):
            self.arrive()
            total = self.w[hi, lo, z]
            for j in range(n_z - 1):
                total = total + self.rz[j]
            place = self.out.at[hi, lo, z, :, :, own_half(None)]
            place[...] = total
            for p in z_peers:
                self.go(place, place, z_dev(p))

        def stage5(self):
            self.arrive()
            place = self.out.at[hi, lo, :, :, :, own_half(0)]
            for p in hi_peers:
                self.go(place, place, hi_dev(p))
            place = self.out.at[hi, lo, :, :, :, own_half(1)]
            for p in lo_peers:
                self.go(place, place, lo_dev(p))

        def stage6(self):
            self.arrive()
            place = self.out.at[:, lo, :, :, :, own_half(0)]
            for p in lo_peers:
                self.go(place, place, lo_dev(p))
            place = self.out.at[hi, :, :, :, :, own_half(1)]
            for p in hi_peers:
                self.go(place, place, hi_dev(p))

        def stage7(self):
            self.arrive()
            place = self.out.at[:, :, :, :, :, own_half(None)]
            self.go(place, place, sibling)

        def stage8(self):
            self.arrive()

    def fill_tap(k, acc_, side):
        total = None
        lhs = jnp.concatenate([n_t[s] for s in range(segs)], axis=1)
        total = jnp.dot(lhs, g3[k, side], preferred_element_type=F32)
        acc_[side] = tiles(total, acc_.shape[1:])

    pool32 = pool16.astype(F32)
    proj_t = lax.dot_general(
        projected_grad,
        pool32,
        (((0,), (0,)), ((), ())),
        precision=HIGHEST,
        preferred_element_type=F32,
    )
    proj_sides = tiles(proj_t[:, :half], pacc.shape[1:]), tiles(proj_t[:, half:], pacc.shape[1:])
    pacc[0] = proj_sides[0]
    pacc[1] = proj_sides[1]

    chunks = [
        Chunk(
            functools.partial(fill_tap, k),
            acc.at[k],
            work.at[k],
            r_a1.at[k],
            r_b1.at[k],
            r_a2.at[k],
            r_b2.at[k],
            r_z.at[k],
            taps_out.at[k],
        )
        for k in range(n_taps)
    ]
    chunks.append(
        Chunk(lambda acc_, side: None, pacc, pwork, pr_a1, pr_b1, pr_a2, pr_b2, pr_z, proj_out)
    )

    gain_state = {"sum": jnp.zeros((8, chans), F32), "moves": []}
    n_pieces = segs // BLOCK_SEGS

    def gain_piece(p):
        rows = slice(p * block, (p + 1) * block)
        lhs = jnp.concatenate(
            [g3[k, side, rows, :] for k in range(n_taps) for side in range(2)], axis=1
        )
        rhs = jnp.concatenate([w_ref[k] for k in range(n_taps)], axis=1)
        back = lax.dot_general(lhs, rhs, contract, preferred_element_type=F32)
        term = back * unit[p * BLOCK_SEGS : (p + 1) * BLOCK_SEGS].reshape(block, chans)
        gain_state["sum"] = gain_state["sum"] + term.reshape(block // 8, 8, chans).sum(axis=0)

    def gain_hop(buffer, index, devices):
        for move in gain_state["moves"]:
            move.wait_recv()
        buffer[index] = gain_state["sum"]
        gain_state["moves"] = [
            links.send(buffer.at[index], buffer.at[index], device) for device in devices
        ]
        gain_state["buffer"] = buffer

    def gain_sum():
        for move in gain_state["moves"]:
            move.wait_recv()
        gain_state["moves"] = []
        buffer = gain_state["buffer"]
        total = buffer[0]
        for j in range(1, buffer.shape[0]):
            total = total + buffer[j]
        gain_state["sum"] = total

    def gain_first():
        gain_state["sum"] = jnp.broadcast_to(
            jnp.sum(gain_state["sum"], axis=0, keepdims=True), (8, chans)
        )
        gain_hop(gc, core, [sibling])

    def gain_lo():
        gain_sum()
        gain_hop(gl, lo, [lo_dev(p) for p in lo_peers])

    def gain_hi():
        gain_sum()
        gain_hop(gh, hi, [hi_dev(p) for p in hi_peers])

    def gain_z():
        gain_sum()
        gain_hop(gz, z, [z_dev(p) for p in z_peers])

    def gain_end():
        gain_sum()
        gain_out[...] = gain_state["sum"]

    extras = [functools.partial(gain_piece, p) for p in range(n_pieces)]
    extras += [gain_first, gain_lo, gain_hi, gain_z, gain_end]

    n_stages = 9
    for step in range(n_stages + len(chunks) - 1):
        for c, chunk in enumerate(chunks):
            stage = step - c
            if 0 <= stage < n_stages:
                getattr(chunk, "stage" + str(stage))()
        if step >= 2 and extras:
            extras.pop(0)()
    while extras:
        extras.pop(0)()
    for copy in links.copies:
        copy.wait_send()


def body(mesh_sizes, segments, conv_weight, gain, head, group, positive):
    n_row, n_grp = mesh_sizes
    n_lo = 2
    n_hi, n_z = n_row // n_lo, n_grp // 2
    shards = n_hi * n_lo * n_z
    records = segments[0]
    segs, length, chans = records.shape
    n_taps = conv_weight.shape[0]
    proj = head.shape[1]
    half, quarter = chans // 2, chans // 4
    count = n_row * segs
    hot = (group[0][:, None] == jnp.arange(proj, dtype=jnp.int32)[None, :]).astype(F32)
    pos = jnp.broadcast_to(positive[0][:, None], (segs, count))
    t = -(-chans // (8 * shards))
    tp = -(-proj // (8 * shards))

    def chunk_shapes(t, lead):
        grid = (n_hi, n_lo, n_z, t, 8)
        return [
            pltpu.VMEM(lead + (2,) + grid + (half,), F32),
            pltpu.VMEM(lead + grid + (half,), F32),
            pltpu.VMEM(lead + (n_lo - 1, n_hi, n_z, t, 8, quarter), F32),
            pltpu.VMEM(lead + (n_hi - 1, n_lo, n_z, t, 8, quarter), F32),
            pltpu.VMEM(lead + (n_hi - 1, n_z, t, 8, quarter), F32),
            pltpu.VMEM(lead + (n_lo - 1, n_z, t, 8, quarter), F32),
            pltpu.VMEM(lead + (n_z - 1, t, 8, half), F32),
        ]

    peers = (n_lo - 1) + (n_hi - 1)
    copies = (n_taps + 1) * 2 * (1 + 2 * peers + n_z - 1)
    copies += (n_row - 1) + 1 + peers + n_z - 1
    rows = segs * length
    scratch = [
        pltpu.VMEM((BLOCK_SEGS * length, n_taps * chans), BF16),
        pltpu.VMEM((BLOCK_SEGS * length, chans), F32),
        pltpu.VMEM((segs, chans, length), BF16),
        pltpu.VMEM((segs, length, chans), F32),
        pltpu.VMEM((segs, length, chans), F32),
        pltpu.VMEM((segs, chans), F32),
        pltpu.VMEM((segs, chans), F32),
        pltpu.VMEM((n_taps, 2, rows, half), BF16),
        pltpu.VMEM((n_row, segs, 2 * proj), F32),
        *chunk_shapes(t, (n_taps,)),
        *chunk_shapes(tp, ()),
        pltpu.VMEM((2, 8, chans), F32),
        pltpu.VMEM((n_lo, 8, chans), F32),
        pltpu.VMEM((n_hi, 8, chans), F32),
        pltpu.VMEM((n_z, 8, chans), F32),
        pltpu.SemaphoreType.DMA((copies,)),
        pltpu.SemaphoreType.DMA((copies,)),
    ]
    vmem = pl.BlockSpec(memory_space=pltpu.VMEM)
    flops = 3 * 2 * rows * chans * chans * n_taps
    taps, projector, gains = pl.pallas_call(
        functools.partial(kernel, (n_row, n_grp, n_hi, n_lo, n_z, count * n_grp)),
        out_shape=(
            jax.ShapeDtypeStruct((n_taps, n_hi, n_lo, n_z, t, 8, chans), F32),
            jax.ShapeDtypeStruct((n_hi, n_lo, n_z, tp, 8, chans), F32),
            jax.ShapeDtypeStruct((8, chans), F32),
        ),
        in_specs=[vmem] * 6,
        out_specs=(vmem,) * 3,
        scratch_shapes=scratch,
        compiler_params=pltpu.CompilerParams(
            collective_id=0, has_side_effects=True, vmem_limit_bytes=60 * 1024 * 1024
        ),
        cost_estimate=pl.CostEstimate(
            flops=flops, bytes_accessed=8 * 1024 * 1024, transcendentals=rows * chans
        ),
    )(records, conv_weight, gain[None, :], head, hot, pos)
    grad_conv = taps.reshape(n_taps, shards * t * 8, chans)[:, :chans]
    projector = projector.reshape(shards * tp * 8, chans)[:proj].T
    return grad_conv, gains[0], projector


def solution(mesh):
    placed = (P("grp", "row", None, None), P(), P(), P(), P("grp", "row"), P("grp", "row"))
    return jax.shard_map(
        functools.partial(body, (mesh.shape["row"], mesh.shape["grp"])),
        mesh=mesh,
        in_specs=placed,
        out_specs=(P(), P(), P()),
        check_vma=False,
    )
```

```python
import functools
import math

import jax
import jax.numpy as jnp
from jax import lax
from jax.experimental import pallas as pl
from jax.experimental.pallas import tpu as pltpu
from jax.sharding import PartitionSpec as P

DILATION_GAP = 2
LOGIT_DIVISOR = 0.1
EPS = 1e-05
GELU_A = math.sqrt(2.0 / math.pi)
GELU_B = 0.044715
HIGHEST = lax.Precision.HIGHEST
MESH = pl.DeviceIdType.MESH
F32 = jnp.float32
BF16 = jnp.bfloat16
BLOCK_SEGS = 4
PARTS = 2


class Links:
    def __init__(self, send_sem, recv_sem):
        self.send_sem, self.recv_sem, self.count, self.copies = send_sem, recv_sem, 0, []

    def send(self, src, dst, device):
        copy = pltpu.make_async_remote_copy(
            src_ref=src,
            dst_ref=dst,
            send_sem=self.send_sem.at[self.count],
            recv_sem=self.recv_sem.at[self.count],
            device_id=device,
            device_id_type=MESH,
        )
        copy.start()
        self.count += 1
        self.copies.append(copy)
        return copy


def shift_rows(values, by, length):
    moved = pltpu.roll(values, by % length, 0)
    edge = moved[:8] if by > 0 else moved[length - 8 :]
    time = lax.broadcasted_iota(jnp.int32, edge.shape, 0)
    edge = jnp.where((time >= by) if by > 0 else (time < 8 + by), edge, 0.0)
    pieces = [edge, moved[8:]] if by > 0 else [moved[: length - 8], edge]
    return jnp.concatenate(pieces, axis=0)


def as_column(line):
    n = line.shape[1]
    square = lax.broadcasted_iota(jnp.int32, (n, n), 0) == lax.broadcasted_iota(
        jnp.int32, (n, n), 1
    )
    return jnp.sum(jnp.where(square, line.astype(F32), 0.0), axis=1, keepdims=True)


def kernel(
    dims,
    seg_hbm,
    w_hbm,
    gain_ref,
    head_ref,
    group_ref,
    pos_ref,
    taps_out,
    proj_out,
    gain_out,
    seg_ref,
    w_ref,
    x3,
    conv,
    n_t,
    unit,
    dgelu,
    pooled,
    hgrad,
    g3,
    embeds,
    acc,
    work,
    r_a1,
    r_b1,
    r_a2,
    r_b2,
    r_z,
    full,
    pacc,
    pwork,
    pr_a1,
    pr_b1,
    pr_a2,
    pr_b2,
    pr_z,
    pfull,
    gc,
    gl,
    gh,
    gz,
    send_sem,
    recv_sem,
    load_sem,
    store_sem,
):
    n_row, n_grp, n_hi, n_lo, n_z, total_segments = dims
    segs, length, chans = seg_ref.shape
    proj = head_ref.shape[1]
    n_taps = w_ref.shape[0]
    half = chans // 2
    quarter = chans // 4
    row = lax.axis_index("row")
    grp = lax.axis_index("grp")
    hi, lo = lax.div(row, n_lo), lax.rem(row, n_lo)
    z, core = lax.div(grp, 2), lax.rem(grp, 2)
    links = Links(send_sem, recv_sem)

    sibling = (row, z * 2 + (1 - core))
    row_peers = [(lax.rem(row + j, n_row), grp) for j in range(1, n_row)]
    lo_peers = [(lax.rem(lo + j, n_lo)) for j in range(1, n_lo)]
    hi_peers = [(lax.rem(hi + j, n_hi)) for j in range(1, n_hi)]
    z_peers = [(lax.rem(z + j, n_z)) for j in range(1, n_z)]

    def lo_dev(p):
        return (hi * n_lo + p, grp)

    def hi_dev(p):
        return (p * n_lo + lo, grp)

    def z_dev(p):
        return (row, p * 2 + core)

    barrier = pltpu.get_barrier_semaphore()
    everyone = [sibling] + row_peers + [z_dev(p) for p in z_peers]
    for device in everyone:
        pl.semaphore_signal(barrier, inc=1, device_id=device, device_id_type=MESH)

    block = BLOCK_SEGS * length
    n_blocks = segs // BLOCK_SEGS

    def seg_load(b):
        part = pl.ds(b * BLOCK_SEGS, BLOCK_SEGS)
        return pltpu.make_async_copy(seg_hbm.at[part], seg_ref.at[part], load_sem.at[b])

    w_load = pltpu.make_async_copy(w_hbm, w_ref, load_sem.at[n_blocks])
    seg_load(0).start()
    w_load.start()
    for b in range(1, n_blocks):
        seg_load(b).start()
    group_one = as_column(group_ref[...]).astype(jnp.int32)
    hot = jnp.where(
        group_one == lax.broadcasted_iota(jnp.int32, (segs, proj), 1), 1.0, 0.0
    ).astype(F32)
    embeds[row, :, proj:] = hot
    w_load.wait()

    @pl.loop(0, n_blocks)
    def _(b):
        seg_load(b).wait()

        @pl.loop(0, BLOCK_SEGS)
        def _(i):
            s = b * BLOCK_SEGS + i
            inputs = seg_ref[s].astype(F32)
            scale = lax.rsqrt(jnp.mean(inputs * inputs, axis=-1, keepdims=True) + EPS)
            normal = inputs * scale
            unit[s] = normal
            normed = normal * gain_ref[...]
            rows = pl.ds(pl.multiple_of(i * length, length), length)
            x3[rows, 0:chans] = shift_rows(normed, DILATION_GAP, length).astype(BF16)
            x3[rows, chans : 2 * chans] = normed.astype(BF16)
            x3[rows, 2 * chans : 3 * chans] = shift_rows(normed, -DILATION_GAP, length).astype(BF16)
            n_t[s] = normed.T.astype(BF16)

        conv[...] = jnp.dot(
            x3[...], w_ref[...].reshape(n_taps * chans, chans), preferred_element_type=F32
        )

        @pl.loop(0, BLOCK_SEGS)
        def _(i):
            s = b * BLOCK_SEGS + i
            total = jnp.zeros((8, chans), F32)
            step = 32
            for q in range(length // step):
                rows = pl.ds(pl.multiple_of(i * length + q * step, step), step)
                v = conv[rows, :]
                v2 = v * v
                th = jnp.tanh(GELU_A * (v + GELU_B * (v2 * v)))
                cdf = 0.5 * (1.0 + th)
                hidden = seg_ref[s, q * step : (q + 1) * step].astype(F32) + v * cdf
                dgelu[s, q * step : (q + 1) * step] = cdf + (0.5 * GELU_A) * v * (
                    1.0 - th * th
                ) * (1.0 + (3.0 * GELU_B) * v2)
                total = total + hidden.reshape(step // 8, 8, chans).sum(axis=0)
            pooled[pl.ds(s, 1), :] = jnp.sum(total, axis=0, keepdims=True) * (1.0 / length)

    pool16 = pooled[...].astype(BF16)
    projected = jnp.dot(pool16, head_ref[...], preferred_element_type=F32)
    inv = lax.rsqrt(jnp.mean(projected * projected, axis=-1, keepdims=True) + EPS)
    embed = projected * inv * proj ** (-0.5)
    embeds[row, :, 0:proj] = embed
    pl.semaphore_wait(barrier, len(everyone))
    moves = [links.send(embeds.at[row], embeds.at[row], device) for device in row_peers]
    for move in moves:
        move.wait_recv()
    every = embeds[...].reshape(n_row * segs, 2 * proj)
    e_all, hot_all = every[:, :proj], every[:, proj:]
    count = n_row * segs
    contract = (((1,), (1,)), ((), ()))

    def scores_of(left):
        return (
            lax.dot_general(left, e_all, contract, precision=HIGHEST, preferred_element_type=F32)
            / LOGIT_DIVISOR
        )

    def same_of(left, first):
        match = lax.dot_general(left, hot_all, contract, preferred_element_type=F32)
        shape = match.shape
        own = first + lax.broadcasted_iota(jnp.int32, shape, 0)
        return jnp.where(own != lax.broadcasted_iota(jnp.int32, shape, 1), match, 0.0)

    s_full, m_full = scores_of(e_all), same_of(hot_all, 0)
    log_row = jnp.log(
        jnp.sum(jnp.where(m_full > 0.5, jnp.exp(s_full), 0.0), axis=0, keepdims=True)
    )
    s_own, m_own = scores_of(embed), same_of(hot, row * segs) > 0.5
    log_own = jnp.log(jnp.sum(jnp.where(m_own, jnp.exp(s_own), 0.0), axis=1, keepdims=True))
    mix = jnp.where(m_own, jnp.exp(s_own - log_own) + jnp.exp(s_own - log_row), 0.0)
    mix = mix - jnp.where(
        as_column(pos_ref[...]).astype(jnp.int32)
        == lax.broadcasted_iota(jnp.int32, (segs, count), 1),
        2.0,
        0.0,
    )
    embed_grad = (total_segments ** (-0.5) / LOGIT_DIVISOR) * jnp.dot(
        mix, e_all, precision=HIGHEST, preferred_element_type=F32
    )
    inner = jnp.mean(embed_grad * projected, axis=-1, keepdims=True)
    projected_grad = proj ** (-0.5) * (embed_grad * inv - projected * (inv * inv * inv * inner))
    hgrad[...] = (
        lax.dot_general(
            projected_grad,
            head_ref[...].astype(F32),
            contract,
            precision=HIGHEST,
            preferred_element_type=F32,
        )
        / length
    )

    def tiles(values, like):
        need = math.prod(like[:-1])
        if need > values.shape[0]:
            pad = jnp.zeros((need - values.shape[0], values.shape[1]), F32)
            values = jnp.concatenate([values, pad], axis=0)
        return values.reshape(like)

    class Chunk:
        def __init__(self, fill, finish, buffers):
            self.fill, self.finish = fill, finish
            self.acc, self.w, self.ra1, self.rb1, self.ra2, self.rb2, self.rz, self.out = buffers
            self.moves = []

        def arrive(self):
            for move in self.moves:
                move.wait_recv()
            self.moves = []

        def go(self, src, dst, device):
            self.moves.append(links.send(src, dst, device))

        def stage0(self):
            self.fill(self.acc, 1 - core)
            self.go(self.acc.at[1 - core], self.w, sibling)
            self.fill(self.acc, core)

        def stage1(self):
            self.arrive()
            w = self.w
            w[...] = w[...] + self.acc[core]
            for j, p in enumerate(lo_peers):
                self.go(w.at[0, :, p], self.ra1.at[j], lo_dev(p))
            for j, p in enumerate(hi_peers):
                self.go(w.at[1, p], self.rb1.at[j], hi_dev(p))

        def stage2(self):
            self.arrive()
            w = self.w
            a = w[0, :, lo]
            for j in range(n_lo - 1):
                a = a + self.ra1[j]
            w[0, :, lo] = a
            b = w[1, hi]
            for j in range(n_hi - 1):
                b = b + self.rb1[j]
            w[1, hi] = b
            for j, p in enumerate(hi_peers):
                self.go(w.at[0, p, lo], self.ra2.at[j], hi_dev(p))
            for j, p in enumerate(lo_peers):
                self.go(w.at[1, hi, p], self.rb2.at[j], lo_dev(p))

        def stage3(self):
            self.arrive()
            w = self.w
            a = w[0, hi, lo]
            for j in range(n_hi - 1):
                a = a + self.ra2[j]
            w[0, hi, lo] = a
            b = w[1, hi, lo]
            for j in range(n_lo - 1):
                b = b + self.rb2[j]
            w[1, hi, lo] = b
            for j, p in enumerate(z_peers):
                self.go(w.at[:, hi, lo, p], self.rz.at[j], z_dev(p))

        def stage4(self):
            self.arrive()
            total = self.w[:, hi, lo, z]
            for j in range(n_z - 1):
                total = total + self.rz[j]
            self.out[core, :, hi, lo, z] = total
            place = self.out.at[core, :, hi, lo, z]
            for p in z_peers:
                self.go(place, place, z_dev(p))

        def stage5(self):
            self.arrive()
            place = self.out.at[core, 0, hi, lo]
            for p in hi_peers:
                self.go(place, place, hi_dev(p))
            place = self.out.at[core, 1, hi, lo]
            for p in lo_peers:
                self.go(place, place, lo_dev(p))

        def stage6(self):
            self.arrive()
            place = self.out.at[core, 0, :, lo]
            for p in lo_peers:
                self.go(place, place, lo_dev(p))
            place = self.out.at[core, 1, hi]
            for p in hi_peers:
                self.go(place, place, hi_dev(p))

        def stage7(self):
            self.arrive()
            place = self.out.at[core]
            self.go(place, place, sibling)

        def stage8(self):
            self.arrive()
            self.finish()

    def put(acc_, side, values):
        for part in range(2):
            acc_[side, part] = tiles(
                values[:, part * quarter : (part + 1) * quarter], acc_.shape[2:]
            )

    parts = acc.shape[0] // n_taps
    part_rows = chans // parts

    def fill_tap(c, acc_, side):
        k, part = c // parts, c % parts
        first = part * part_rows
        lhs = jnp.concatenate([n_t[s, first : first + part_rows] for s in range(segs)], axis=1)
        put(acc_, side, jnp.dot(lhs, g3[k, side], preferred_element_type=F32))

    stores = []

    def store_tap(c):
        for side in range(2):
            for part in range(2):
                first = side * half + part * quarter
                store = pltpu.make_async_copy(
                    full.at[c, side, part],
                    taps_out.at[c, :, :, :, :, :, pl.ds(first, quarter)],
                    store_sem.at[len(stores)],
                )
                store.start()
                stores.append(store)

    def store_proj():
        for side in range(2):
            for part in range(2):
                first = side * half + part * quarter
                block_t = pfull[side, part].reshape(-1, quarter)[:proj]
                proj_out[first : first + quarter, :] = block_t.T

    pool32 = pool16.astype(F32)
    proj_t = lax.dot_general(
        projected_grad,
        pool32,
        (((0,), (0,)), ((), ())),
        precision=HIGHEST,
        preferred_element_type=F32,
    )
    for side in range(2):
        put(pacc, side, proj_t[:, side * half : (side + 1) * half])

    proj_buffers = (pacc, pwork, pr_a1, pr_b1, pr_a2, pr_b2, pr_z, pfull)
    tap_buffers = (acc, work, r_a1, r_b1, r_a2, r_b2, r_z, full)
    chunks = [Chunk(lambda acc_, side: None, store_proj, proj_buffers)]
    chunks += [
        Chunk(
            functools.partial(fill_tap, c),
            functools.partial(store_tap, c),
            [buffer.at[c] for buffer in tap_buffers],
        )
        for c in range(n_taps * parts)
    ]
    chunks[0].stage0()

    @pl.loop(0, segs)
    def _(s):
        grad = (dgelu[s] * hgrad[pl.ds(s, 1), :]).astype(BF16)
        grad32 = grad.astype(F32)
        rows = pl.ds(pl.multiple_of(s * length, length), length)
        shifted = (
            shift_rows(grad32, -DILATION_GAP, length).astype(BF16),
            grad,
            shift_rows(grad32, DILATION_GAP, length).astype(BF16),
        )
        for k in range(n_taps):
            g3[k, 0, rows, :] = shifted[k][:, :half]
            g3[k, 1, rows, :] = shifted[k][:, half:]

    gain_state = {"sum": jnp.zeros((8, chans), F32), "moves": []}
    n_pieces = segs // BLOCK_SEGS

    def gain_piece(p):
        rows = slice(p * block, (p + 1) * block)
        lhs = jnp.concatenate(
            [g3[k, side, rows, :] for k in range(n_taps) for side in range(2)], axis=1
        )
        rhs = jnp.concatenate([w_ref[k] for k in range(n_taps)], axis=1)
        back = lax.dot_general(lhs, rhs, contract, preferred_element_type=F32)
        term = back * unit[p * BLOCK_SEGS : (p + 1) * BLOCK_SEGS].reshape(block, chans)
        gain_state["sum"] = gain_state["sum"] + term.reshape(block // 8, 8, chans).sum(axis=0)

    def gain_hop(buffer, index, devices):
        for move in gain_state["moves"]:
            move.wait_recv()
        buffer[index] = gain_state["sum"]
        gain_state["moves"] = [
            links.send(buffer.at[index], buffer.at[index], device) for device in devices
        ]
        gain_state["buffer"] = buffer

    def gain_sum():
        for move in gain_state["moves"]:
            move.wait_recv()
        gain_state["moves"] = []
        buffer = gain_state["buffer"]
        total = buffer[0]
        for j in range(1, buffer.shape[0]):
            total = total + buffer[j]
        gain_state["sum"] = total

    def gain_first():
        gain_state["sum"] = jnp.broadcast_to(
            jnp.sum(gain_state["sum"], axis=0, keepdims=True), (8, chans)
        )
        gain_hop(gc, core, [sibling])

    def gain_lo():
        gain_sum()
        gain_hop(gl, lo, [lo_dev(p) for p in lo_peers])

    def gain_hi():
        gain_sum()
        gain_hop(gh, hi, [hi_dev(p) for p in hi_peers])

    def gain_z():
        gain_sum()
        gain_hop(gz, z, [z_dev(p) for p in z_peers])

    def gain_end():
        gain_sum()
        gain_out[...] = gain_state["sum"][:1]

    extras = [functools.partial(gain_piece, p) for p in range(n_pieces)]
    extras += [gain_first, gain_lo, gain_hi, gain_z, gain_end]

    n_stages = 9
    for step in range(n_stages + len(chunks) - 1):
        for c, chunk in enumerate(chunks):
            stage = step - c
            if 0 <= stage < n_stages and (step > 0 or c > 0):
                getattr(chunk, "stage" + str(stage))()
        if step >= 2 and extras:
            extras.pop(0)()
    while extras:
        extras.pop(0)()
    for copy in links.copies:
        copy.wait_send()
    for store in stores:
        store.wait()


def place_kernel(taps, projector, gains, taps_out, projector_out, gains_out, sems):
    pairs = [(taps.at[c], taps_out.at[c]) for c in range(taps.shape[0])]
    pairs += [(projector, projector_out), (gains, gains_out)]
    copies = [pltpu.make_async_copy(*pair, sems.at[i]) for i, pair in enumerate(pairs)]
    for copy in copies:
        copy.start()
    for copy in copies:
        copy.wait()


def body(mesh_sizes, segments, conv_weight, gain, head, group, positive):
    n_row, n_grp = mesh_sizes
    n_lo = 2
    n_hi, n_z = n_row // n_lo, n_grp // 2
    shards = n_hi * n_lo * n_z
    records = segments[0]
    segs, length, chans = records.shape
    n_taps = conv_weight.shape[0]
    proj = head.shape[1]
    half, quarter = chans // 2, chans // 4
    count = n_row * segs
    parts = max(1, min(PARTS, chans // (8 * shards)))
    n_chunks = n_taps * parts
    t = -(-chans // (8 * shards * parts))
    tp = -(-proj // (8 * shards))

    def chunk_shapes(t, lead):
        grid = (n_hi, n_lo, n_z, t, 8)
        return [
            pltpu.VMEM(lead + (2, 2) + grid + (quarter,), F32),
            pltpu.VMEM(lead + (2,) + grid + (quarter,), F32),
            pltpu.VMEM(lead + (n_lo - 1, n_hi, n_z, t, 8, quarter), F32),
            pltpu.VMEM(lead + (n_hi - 1, n_lo, n_z, t, 8, quarter), F32),
            pltpu.VMEM(lead + (n_hi - 1, n_z, t, 8, quarter), F32),
            pltpu.VMEM(lead + (n_lo - 1, n_z, t, 8, quarter), F32),
            pltpu.VMEM(lead + (n_z - 1, 2, t, 8, quarter), F32),
            pltpu.VMEM(lead + (2, 2) + grid + (quarter,), F32),
        ]

    peers = (n_lo - 1) + (n_hi - 1)
    copies = (n_chunks + 1) * 2 * (1 + 2 * peers + n_z - 1)
    copies += (n_row - 1) + 1 + peers + n_z - 1
    rows = segs * length
    scratch = [
        pltpu.VMEM(records.shape, BF16),
        pltpu.VMEM(conv_weight.shape, BF16),
        pltpu.VMEM((BLOCK_SEGS * length, n_taps * chans), BF16),
        pltpu.VMEM((BLOCK_SEGS * length, chans), F32),
        pltpu.VMEM((segs, chans, length), BF16),
        pltpu.VMEM((segs, length, chans), F32),
        pltpu.VMEM((segs, length, chans), F32),
        pltpu.VMEM((segs, chans), F32),
        pltpu.VMEM((segs, chans), F32),
        pltpu.VMEM((n_taps, 2, rows, half), BF16),
        pltpu.VMEM((n_row, segs, 2 * proj), F32),
        *chunk_shapes(t, (n_chunks,)),
        *chunk_shapes(tp, ()),
        pltpu.VMEM((2, 8, chans), F32),
        pltpu.VMEM((n_lo, 8, chans), F32),
        pltpu.VMEM((n_hi, 8, chans), F32),
        pltpu.VMEM((n_z, 8, chans), F32),
        pltpu.SemaphoreType.DMA((copies,)),
        pltpu.SemaphoreType.DMA((copies,)),
        pltpu.SemaphoreType.DMA((segs // BLOCK_SEGS + 1,)),
        pltpu.SemaphoreType.DMA((n_chunks * 4,)),
    ]
    vmem = pl.BlockSpec(memory_space=pltpu.VMEM)
    anywhere = pl.BlockSpec(memory_space=pl.ANY)
    flops = 3 * 2 * rows * chans * chans * n_taps
    taps, projector, gains = pl.pallas_call(
        functools.partial(kernel, (n_row, n_grp, n_hi, n_lo, n_z, count * n_grp)),
        out_shape=(
            jax.ShapeDtypeStruct((n_chunks, n_hi, n_lo, n_z, t, 8, chans), F32),
            jax.ShapeDtypeStruct((chans, proj), F32),
            jax.ShapeDtypeStruct((1, chans), F32),
        ),
        in_specs=[anywhere] * 2 + [vmem] * 4,
        out_specs=(anywhere, vmem, vmem),
        scratch_shapes=scratch,
        compiler_params=pltpu.CompilerParams(
            collective_id=0, has_side_effects=True, vmem_limit_bytes=60 * 1024 * 1024
        ),
        cost_estimate=pl.CostEstimate(
            flops=flops, bytes_accessed=8 * 1024 * 1024, transcendentals=rows * chans
        ),
    )(records, conv_weight, gain[None, :], head, group, positive)
    results = (taps, projector, gains)
    taps, projector, gains = pl.pallas_call(
        place_kernel,
        out_shape=tuple(jax.ShapeDtypeStruct(r.shape, F32) for r in results),
        in_specs=[anywhere] * 3,
        out_specs=(anywhere,) * 3,
        scratch_shapes=[pltpu.SemaphoreType.DMA((n_chunks + 2,))],
        compiler_params=pltpu.CompilerParams(vmem_limit_bytes=60 * 1024 * 1024),
    )(*results)
    rows_each = chans // parts
    taps = taps.reshape(n_chunks, shards * t * 8, chans)[:, :rows_each]
    return taps.reshape(n_taps, chans, chans), gains.reshape(chans), projector


def solution(mesh):
    placed = (P("grp", "row", None, None), P(), P(), P(), P("grp", "row"), P("grp", "row"))
    return jax.shard_map(
        functools.partial(body, (mesh.shape["row"], mesh.shape["grp"])),
        mesh=mesh,
        in_specs=placed,
        out_specs=(P(), P(), P()),
        check_vma=False,
    )
```

```python
import functools
import math

import jax
import jax.numpy as jnp
from jax import lax
from jax.experimental import pallas as pl
from jax.experimental.pallas import tpu as pltpu
from jax.sharding import PartitionSpec as P

DILATION_GAP = 2
LOGIT_DIVISOR = 0.1
EPS = 1e-05
GELU_A = math.sqrt(2.0 / math.pi)
GELU_B = 0.044715
HIGHEST = lax.Precision.HIGHEST
MESH = pl.DeviceIdType.MESH
F32 = jnp.float32
BF16 = jnp.bfloat16
BLOCK_SEGS = 4
PARTS = 1
PLACE_ROWS = 256


class Links:
    def __init__(self, send_sem, recv_sem):
        self.send_sem, self.recv_sem, self.count, self.copies = send_sem, recv_sem, 0, []

    def send(self, src, dst, device):
        copy = pltpu.make_async_remote_copy(
            src_ref=src,
            dst_ref=dst,
            send_sem=self.send_sem.at[self.count],
            recv_sem=self.recv_sem.at[self.count],
            device_id=device,
            device_id_type=MESH,
        )
        copy.start()
        self.count += 1
        self.copies.append(copy)
        return copy


def shift_rows(values, by, length):
    moved = pltpu.roll(values, by % length, 0)
    edge = moved[:8] if by > 0 else moved[length - 8 :]
    time = lax.broadcasted_iota(jnp.int32, edge.shape, 0)
    edge = jnp.where((time >= by) if by > 0 else (time < 8 + by), edge, 0.0)
    pieces = [edge, moved[8:]] if by > 0 else [moved[: length - 8], edge]
    return jnp.concatenate(pieces, axis=0)


def as_column(line):
    n = line.shape[1]
    square = lax.broadcasted_iota(jnp.int32, (n, n), 0) == lax.broadcasted_iota(
        jnp.int32, (n, n), 1
    )
    return jnp.sum(jnp.where(square, line.astype(F32), 0.0), axis=1, keepdims=True)


def kernel(
    dims,
    seg_hbm,
    w_hbm,
    gain_ref,
    head_ref,
    group_ref,
    pos_ref,
    taps_out,
    proj_out,
    gain_out,
    seg_ref,
    w_ref,
    x3,
    conv,
    n_t,
    unit,
    dgelu,
    pooled,
    hgrad,
    g3,
    embeds,
    acc,
    work,
    r_a1,
    r_b1,
    r_a2,
    r_b2,
    r_z,
    full,
    pacc,
    pwork,
    pr_a1,
    pr_b1,
    pr_a2,
    pr_b2,
    pr_z,
    pfull,
    gc,
    gl,
    gh,
    gz,
    send_sem,
    recv_sem,
    load_sem,
    store_sem,
):
    n_row, n_grp, n_hi, n_lo, n_z, total_segments = dims
    segs, length, chans = seg_ref.shape
    proj = head_ref.shape[1]
    n_taps = w_ref.shape[0]
    half = chans // 2
    quarter = chans // 4
    row = lax.axis_index("row")
    grp = lax.axis_index("grp")
    hi, lo = lax.div(row, n_lo), lax.rem(row, n_lo)
    z, core = lax.div(grp, 2), lax.rem(grp, 2)
    links = Links(send_sem, recv_sem)

    sibling = (row, z * 2 + (1 - core))
    row_peers = [(lax.rem(row + j, n_row), grp) for j in range(1, n_row)]
    lo_peers = [(lax.rem(lo + j, n_lo)) for j in range(1, n_lo)]
    hi_peers = [(lax.rem(hi + j, n_hi)) for j in range(1, n_hi)]
    z_peers = [(lax.rem(z + j, n_z)) for j in range(1, n_z)]

    def lo_dev(p):
        return (hi * n_lo + p, grp)

    def hi_dev(p):
        return (p * n_lo + lo, grp)

    def z_dev(p):
        return (row, p * 2 + core)

    barrier = pltpu.get_barrier_semaphore()
    everyone = [sibling] + row_peers + [z_dev(p) for p in z_peers]
    for device in everyone:
        pl.semaphore_signal(barrier, inc=1, device_id=device, device_id_type=MESH)

    block = BLOCK_SEGS * length
    n_blocks = segs // BLOCK_SEGS

    def seg_load(b):
        part = pl.ds(b * BLOCK_SEGS, BLOCK_SEGS)
        return pltpu.make_async_copy(seg_hbm.at[part], seg_ref.at[part], load_sem.at[b])

    w_load = pltpu.make_async_copy(w_hbm, w_ref, load_sem.at[n_blocks])
    seg_load(0).start()
    w_load.start()
    for b in range(1, n_blocks):
        seg_load(b).start()
    group_one = as_column(group_ref[...]).astype(jnp.int32)
    hot = jnp.where(
        group_one == lax.broadcasted_iota(jnp.int32, (segs, proj), 1), 1.0, 0.0
    ).astype(F32)
    embeds[row, :, proj:] = hot
    w_load.wait()

    @pl.loop(0, n_blocks)
    def _(b):
        seg_load(b).wait()

        @pl.loop(0, BLOCK_SEGS)
        def _(i):
            s = b * BLOCK_SEGS + i
            inputs = seg_ref[s].astype(F32)
            scale = lax.rsqrt(jnp.mean(inputs * inputs, axis=-1, keepdims=True) + EPS)
            normal = inputs * scale
            unit[s] = normal
            normed = normal * gain_ref[...]
            rows = pl.ds(pl.multiple_of(i * length, length), length)
            x3[rows, 0:chans] = shift_rows(normed, DILATION_GAP, length).astype(BF16)
            x3[rows, chans : 2 * chans] = normed.astype(BF16)
            x3[rows, 2 * chans : 3 * chans] = shift_rows(normed, -DILATION_GAP, length).astype(BF16)
            n_t[s] = normed.T.astype(BF16)

        conv[...] = jnp.dot(
            x3[...], w_ref[...].reshape(n_taps * chans, chans), preferred_element_type=F32
        )

        @pl.loop(0, BLOCK_SEGS)
        def _(i):
            s = b * BLOCK_SEGS + i
            total = jnp.zeros((8, chans), F32)
            step = 32
            for q in range(length // step):
                rows = pl.ds(pl.multiple_of(i * length + q * step, step), step)
                v = conv[rows, :]
                v2 = v * v
                th = jnp.tanh(GELU_A * (v + GELU_B * (v2 * v)))
                cdf = 0.5 * (1.0 + th)
                hidden = seg_ref[s, q * step : (q + 1) * step].astype(F32) + v * cdf
                dgelu[s, q * step : (q + 1) * step] = cdf + (0.5 * GELU_A) * v * (
                    1.0 - th * th
                ) * (1.0 + (3.0 * GELU_B) * v2)
                total = total + hidden.reshape(step // 8, 8, chans).sum(axis=0)
            pooled[pl.ds(s, 1), :] = jnp.sum(total, axis=0, keepdims=True) * (1.0 / length)

    pool16 = pooled[...].astype(BF16)
    projected = jnp.dot(pool16, head_ref[...], preferred_element_type=F32)
    inv = lax.rsqrt(jnp.mean(projected * projected, axis=-1, keepdims=True) + EPS)
    embed = projected * inv * proj ** (-0.5)
    embeds[row, :, 0:proj] = embed
    pl.semaphore_wait(barrier, len(everyone))
    moves = [links.send(embeds.at[row], embeds.at[row], device) for device in row_peers]
    for move in moves:
        move.wait_recv()
    every = embeds[...].reshape(n_row * segs, 2 * proj)
    e_all, hot_all = every[:, :proj], every[:, proj:]
    count = n_row * segs
    contract = (((1,), (1,)), ((), ()))

    def scores_of(left):
        return (
            lax.dot_general(left, e_all, contract, precision=HIGHEST, preferred_element_type=F32)
            / LOGIT_DIVISOR
        )

    def same_of(left, first):
        match = lax.dot_general(left, hot_all, contract, preferred_element_type=F32)
        shape = match.shape
        own = first + lax.broadcasted_iota(jnp.int32, shape, 0)
        return jnp.where(own != lax.broadcasted_iota(jnp.int32, shape, 1), match, 0.0)

    s_full, m_full = scores_of(e_all), same_of(hot_all, 0)
    log_row = jnp.log(
        jnp.sum(jnp.where(m_full > 0.5, jnp.exp(s_full), 0.0), axis=0, keepdims=True)
    )
    s_own, m_own = scores_of(embed), same_of(hot, row * segs) > 0.5
    log_own = jnp.log(jnp.sum(jnp.where(m_own, jnp.exp(s_own), 0.0), axis=1, keepdims=True))
    mix = jnp.where(m_own, jnp.exp(s_own - log_own) + jnp.exp(s_own - log_row), 0.0)
    mix = mix - jnp.where(
        as_column(pos_ref[...]).astype(jnp.int32)
        == lax.broadcasted_iota(jnp.int32, (segs, count), 1),
        2.0,
        0.0,
    )
    embed_grad = (total_segments ** (-0.5) / LOGIT_DIVISOR) * jnp.dot(
        mix, e_all, precision=HIGHEST, preferred_element_type=F32
    )
    inner = jnp.mean(embed_grad * projected, axis=-1, keepdims=True)
    projected_grad = proj ** (-0.5) * (embed_grad * inv - projected * (inv * inv * inv * inner))
    hgrad[...] = (
        lax.dot_general(
            projected_grad,
            head_ref[...].astype(F32),
            contract,
            precision=HIGHEST,
            preferred_element_type=F32,
        )
        / length
    )

    def tiles(values, like):
        need = math.prod(like[:-1])
        if need > values.shape[0]:
            pad = jnp.zeros((need - values.shape[0], values.shape[1]), F32)
            values = jnp.concatenate([values, pad], axis=0)
        return values.reshape(like)

    class Chunk:
        def __init__(self, fill, finish, buffers):
            self.fill, self.finish = fill, finish
            self.acc, self.w, self.ra1, self.rb1, self.ra2, self.rb2, self.rz, self.out = buffers
            self.moves = []

        def arrive(self):
            for move in self.moves:
                move.wait_recv()
            self.moves = []

        def go(self, src, dst, device):
            self.moves.append(links.send(src, dst, device))

        def stage0(self):
            self.fill(self.acc, 1 - core)
            self.go(self.acc.at[1 - core], self.w, sibling)
            self.fill(self.acc, core)

        def stage1(self):
            self.arrive()
            w = self.w
            w[...] = w[...] + self.acc[core]
            for j, p in enumerate(lo_peers):
                self.go(w.at[0, :, p], self.ra1.at[j], lo_dev(p))
            for j, p in enumerate(hi_peers):
                self.go(w.at[1, p], self.rb1.at[j], hi_dev(p))

        def stage2(self):
            self.arrive()
            w = self.w
            a = w[0, :, lo]
            for j in range(n_lo - 1):
                a = a + self.ra1[j]
            w[0, :, lo] = a
            b = w[1, hi]
            for j in range(n_hi - 1):
                b = b + self.rb1[j]
            w[1, hi] = b
            for j, p in enumerate(hi_peers):
                self.go(w.at[0, p, lo], self.ra2.at[j], hi_dev(p))
            for j, p in enumerate(lo_peers):
                self.go(w.at[1, hi, p], self.rb2.at[j], lo_dev(p))

        def stage3(self):
            self.arrive()
            w = self.w
            a = w[0, hi, lo]
            for j in range(n_hi - 1):
                a = a + self.ra2[j]
            w[0, hi, lo] = a
            b = w[1, hi, lo]
            for j in range(n_lo - 1):
                b = b + self.rb2[j]
            w[1, hi, lo] = b
            for j, p in enumerate(z_peers):
                self.go(w.at[:, hi, lo, p], self.rz.at[j], z_dev(p))

        def stage4(self):
            self.arrive()
            total = self.w[:, hi, lo, z]
            for j in range(n_z - 1):
                total = total + self.rz[j]
            self.out[core, :, hi, lo, z] = total
            place = self.out.at[core, :, hi, lo, z]
            for p in z_peers:
                self.go(place, place, z_dev(p))

        def stage5(self):
            self.arrive()
            place = self.out.at[core, 0, hi, lo]
            for p in hi_peers:
                self.go(place, place, hi_dev(p))
            place = self.out.at[core, 1, hi, lo]
            for p in lo_peers:
                self.go(place, place, lo_dev(p))

        def stage6(self):
            self.arrive()
            place = self.out.at[core, 0, :, lo]
            for p in lo_peers:
                self.go(place, place, lo_dev(p))
            place = self.out.at[core, 1, hi]
            for p in hi_peers:
                self.go(place, place, hi_dev(p))

        def stage7(self):
            self.arrive()
            place = self.out.at[core]
            self.go(place, place, sibling)

        def stage8(self):
            self.arrive()
            self.finish()

    def put(acc_, side, values):
        for part in range(2):
            acc_[side, part] = tiles(
                values[:, part * quarter : (part + 1) * quarter], acc_.shape[2:]
            )

    parts = acc.shape[0] // n_taps
    part_rows = chans // parts

    def fill_tap(c, acc_, side):
        k, part = c // parts, c % parts
        first = part * part_rows
        lhs = jnp.concatenate([n_t[s, first : first + part_rows] for s in range(segs)], axis=1)
        put(acc_, side, jnp.dot(lhs, g3[k, side], preferred_element_type=F32))

    stores = []

    def store_tap(c):
        for side in range(2):
            for part in range(2):
                first = side * half + part * quarter
                store = pltpu.make_async_copy(
                    full.at[c, side, part],
                    taps_out.at[c, :, :, :, :, :, pl.ds(first, quarter)],
                    store_sem.at[len(stores)],
                )
                store.start()
                stores.append(store)

    def store_proj():
        for side in range(2):
            for part in range(2):
                first = side * half + part * quarter
                block_t = pfull[side, part].reshape(-1, quarter)[:proj]
                proj_out[first : first + quarter, :] = block_t.T

    pool32 = pool16.astype(F32)
    proj_t = lax.dot_general(
        projected_grad,
        pool32,
        (((0,), (0,)), ((), ())),
        precision=HIGHEST,
        preferred_element_type=F32,
    )
    for side in range(2):
        put(pacc, side, proj_t[:, side * half : (side + 1) * half])

    proj_buffers = (pacc, pwork, pr_a1, pr_b1, pr_a2, pr_b2, pr_z, pfull)
    tap_buffers = (acc, work, r_a1, r_b1, r_a2, r_b2, r_z, full)
    chunks = [Chunk(lambda acc_, side: None, store_proj, proj_buffers)]
    chunks += [
        Chunk(
            functools.partial(fill_tap, c),
            functools.partial(store_tap, c),
            [buffer.at[c] for buffer in tap_buffers],
        )
        for c in sorted(range(n_taps * parts), key=lambda c: c // parts != n_taps // 2)
    ]
    chunks[0].stage0()

    middle = n_taps // 2

    @pl.loop(0, segs)
    def _(s):
        grad = (dgelu[s] * hgrad[pl.ds(s, 1), :]).astype(BF16)
        rows = pl.ds(pl.multiple_of(s * length, length), length)
        for side in range(2):
            g3[middle, side, rows, :] = grad[:, side * half : (side + 1) * half]

    def shift_grads():
        @pl.loop(0, segs)
        def _(s):
            rows = pl.ds(pl.multiple_of(s * length, length), length)
            for side in range(2):
                grad = g3[middle, side, rows, :].astype(F32)
                for k in range(n_taps):
                    if k != middle:
                        by = (k - middle) * DILATION_GAP
                        g3[k, side, rows, :] = shift_rows(grad, by, length).astype(BF16)

    gain_state = {"sum": jnp.zeros((8, chans), F32), "moves": []}
    n_pieces = segs // BLOCK_SEGS

    def gain_piece(p):
        rows = slice(p * block, (p + 1) * block)
        lhs = jnp.concatenate(
            [g3[k, side, rows, :] for k in range(n_taps) for side in range(2)], axis=1
        )
        rhs = jnp.concatenate([w_ref[k] for k in range(n_taps)], axis=1)
        back = lax.dot_general(lhs, rhs, contract, preferred_element_type=F32)
        term = back * unit[p * BLOCK_SEGS : (p + 1) * BLOCK_SEGS].reshape(block, chans)
        gain_state["sum"] = gain_state["sum"] + term.reshape(block // 8, 8, chans).sum(axis=0)

    def gain_hop(buffer, index, devices):
        for move in gain_state["moves"]:
            move.wait_recv()
        buffer[index] = gain_state["sum"]
        gain_state["moves"] = [
            links.send(buffer.at[index], buffer.at[index], device) for device in devices
        ]
        gain_state["buffer"] = buffer

    def gain_sum():
        for move in gain_state["moves"]:
            move.wait_recv()
        gain_state["moves"] = []
        buffer = gain_state["buffer"]
        total = buffer[0]
        for j in range(1, buffer.shape[0]):
            total = total + buffer[j]
        gain_state["sum"] = total

    def gain_first():
        gain_state["sum"] = jnp.broadcast_to(
            jnp.sum(gain_state["sum"], axis=0, keepdims=True), (8, chans)
        )
        gain_hop(gc, core, [sibling])

    def gain_lo():
        gain_sum()
        gain_hop(gl, lo, [lo_dev(p) for p in lo_peers])

    def gain_hi():
        gain_sum()
        gain_hop(gh, hi, [hi_dev(p) for p in hi_peers])

    def gain_z():
        gain_sum()
        gain_hop(gz, z, [z_dev(p) for p in z_peers])

    def gain_end():
        gain_sum()
        gain_out[...] = gain_state["sum"][:1]

    extras = [functools.partial(gain_piece, p) for p in range(n_pieces)]
    extras += [gain_first, gain_lo, gain_hi, gain_z, gain_end]

    n_stages = 9
    for step in range(n_stages + len(chunks) - 1):
        for c, chunk in enumerate(chunks):
            stage = step - c
            if 0 <= stage < n_stages and (step > 0 or c > 0):
                getattr(chunk, "stage" + str(stage))()
        if step == parts:
            shift_grads()
        if step >= 3 and extras:
            extras.pop(0)()
    while extras:
        extras.pop(0)()
    for copy in links.copies:
        copy.wait_send()
    for store in stores:
        store.wait()


def place_kernel(taps, projector, gains, taps_out, projector_out, gains_out):
    taps_out[...] = taps[...]
    projector_out[...] = projector[...]
    gains_out[...] = gains[...]


def body(mesh_sizes, segments, conv_weight, gain, head, group, positive):
    n_row, n_grp = mesh_sizes
    n_lo = 2
    n_hi, n_z = n_row // n_lo, n_grp // 2
    shards = n_hi * n_lo * n_z
    records = segments[0]
    segs, length, chans = records.shape
    n_taps = conv_weight.shape[0]
    proj = head.shape[1]
    half, quarter = chans // 2, chans // 4
    count = n_row * segs
    parts = max(1, min(PARTS, chans // (8 * shards)))
    n_chunks = n_taps * parts
    t = -(-chans // (8 * shards * parts))
    tp = -(-proj // (8 * shards))

    def chunk_shapes(t, lead):
        grid = (n_hi, n_lo, n_z, t, 8)
        return [
            pltpu.VMEM(lead + (2, 2) + grid + (quarter,), F32),
            pltpu.VMEM(lead + (2,) + grid + (quarter,), F32),
            pltpu.VMEM(lead + (n_lo - 1, n_hi, n_z, t, 8, quarter), F32),
            pltpu.VMEM(lead + (n_hi - 1, n_lo, n_z, t, 8, quarter), F32),
            pltpu.VMEM(lead + (n_hi - 1, n_z, t, 8, quarter), F32),
            pltpu.VMEM(lead + (n_lo - 1, n_z, t, 8, quarter), F32),
            pltpu.VMEM(lead + (n_z - 1, 2, t, 8, quarter), F32),
            pltpu.VMEM(lead + (2, 2) + grid + (quarter,), F32),
        ]

    peers = (n_lo - 1) + (n_hi - 1)
    copies = (n_chunks + 1) * 2 * (1 + 2 * peers + n_z - 1)
    copies += (n_row - 1) + 1 + peers + n_z - 1
    rows = segs * length
    scratch = [
        pltpu.VMEM(records.shape, BF16),
        pltpu.VMEM(conv_weight.shape, BF16),
        pltpu.VMEM((BLOCK_SEGS * length, n_taps * chans), BF16),
        pltpu.VMEM((BLOCK_SEGS * length, chans), F32),
        pltpu.VMEM((segs, chans, length), BF16),
        pltpu.VMEM((segs, length, chans), F32),
        pltpu.VMEM((segs, length, chans), F32),
        pltpu.VMEM((segs, chans), F32),
        pltpu.VMEM((segs, chans), F32),
        pltpu.VMEM((n_taps, 2, rows, half), BF16),
        pltpu.VMEM((n_row, segs, 2 * proj), F32),
        *chunk_shapes(t, (n_chunks,)),
        *chunk_shapes(tp, ()),
        pltpu.VMEM((2, 8, chans), F32),
        pltpu.VMEM((n_lo, 8, chans), F32),
        pltpu.VMEM((n_hi, 8, chans), F32),
        pltpu.VMEM((n_z, 8, chans), F32),
        pltpu.SemaphoreType.DMA((copies,)),
        pltpu.SemaphoreType.DMA((copies,)),
        pltpu.SemaphoreType.DMA((segs // BLOCK_SEGS + 1,)),
        pltpu.SemaphoreType.DMA((n_chunks * 4,)),
    ]
    vmem = pl.BlockSpec(memory_space=pltpu.VMEM)
    anywhere = pl.BlockSpec(memory_space=pl.ANY)
    flops = 3 * 2 * rows * chans * chans * n_taps
    taps, projector, gains = pl.pallas_call(
        functools.partial(kernel, (n_row, n_grp, n_hi, n_lo, n_z, count * n_grp)),
        out_shape=(
            jax.ShapeDtypeStruct((n_chunks, n_hi, n_lo, n_z, t, 8, chans), F32),
            jax.ShapeDtypeStruct((chans, proj), F32),
            jax.ShapeDtypeStruct((1, chans), F32),
        ),
        in_specs=[anywhere] * 2 + [vmem] * 4,
        out_specs=(anywhere, vmem, vmem),
        scratch_shapes=scratch,
        compiler_params=pltpu.CompilerParams(
            collective_id=0, has_side_effects=True, vmem_limit_bytes=60 * 1024 * 1024
        ),
        cost_estimate=pl.CostEstimate(
            flops=flops, bytes_accessed=8 * 1024 * 1024, transcendentals=rows * chans
        ),
    )(records, conv_weight, gain[None, :], head, group, positive)
    taps = taps.reshape(n_chunks, shards * t * 8, chans)
    rows_each = chans // parts
    pieces = rows_each // PLACE_ROWS
    places = (
        pl.BlockSpec((1, PLACE_ROWS, chans), lambda i: (i // pieces, i % pieces, 0)),
        pl.BlockSpec((chans, proj), lambda i: (0, 0)),
        pl.BlockSpec((1, chans), lambda i: (0, 0)),
    )
    taps, projector, gains = pl.pallas_call(
        place_kernel,
        grid=(n_chunks * pieces,),
        out_shape=(
            jax.ShapeDtypeStruct((n_chunks, rows_each, chans), F32),
            jax.ShapeDtypeStruct((chans, proj), F32),
            jax.ShapeDtypeStruct((1, chans), F32),
        ),
        in_specs=places,
        out_specs=places,
        compiler_params=pltpu.CompilerParams(vmem_limit_bytes=60 * 1024 * 1024),
    )(taps, projector, gains)
    return taps.reshape(n_taps, chans, chans), gains.reshape(chans), projector


def solution(mesh):
    placed = (P("grp", "row", None, None), P(), P(), P(), P("grp", "row"), P("grp", "row"))
    return jax.shard_map(
        functools.partial(body, (mesh.shape["row"], mesh.shape["grp"])),
        mesh=mesh,
        in_specs=placed,
        out_specs=(P(), P(), P()),
        check_vma=False,
    )
```

```python
import functools
import math

import jax
import jax.numpy as jnp
from jax import lax
from jax.experimental import pallas as pl
from jax.experimental.pallas import tpu as pltpu
from jax.sharding import PartitionSpec as P

DILATION_GAP = 2
LOGIT_DIVISOR = 0.1
EPS = 1e-05
GELU_A = math.sqrt(2.0 / math.pi)
GELU_B = 0.044715
HIGHEST = lax.Precision.HIGHEST
MESH = pl.DeviceIdType.MESH
F32 = jnp.float32
BF16 = jnp.bfloat16
BLOCK_SEGS = 4
PARTS = 1


class Links:
    def __init__(self, send_sem, recv_sem):
        self.send_sem, self.recv_sem, self.count, self.copies = send_sem, recv_sem, 0, []

    def send(self, src, dst, device):
        copy = pltpu.make_async_remote_copy(
            src_ref=src,
            dst_ref=dst,
            send_sem=self.send_sem.at[self.count],
            recv_sem=self.recv_sem.at[self.count],
            device_id=device,
            device_id_type=MESH,
        )
        copy.start()
        self.count += 1
        self.copies.append(copy)
        return copy


def shift_rows(values, by, length):
    moved = pltpu.roll(values, by % length, 0)
    edge = moved[:8] if by > 0 else moved[length - 8 :]
    time = lax.broadcasted_iota(jnp.int32, edge.shape, 0)
    edge = jnp.where((time >= by) if by > 0 else (time < 8 + by), edge, 0.0)
    pieces = [edge, moved[8:]] if by > 0 else [moved[: length - 8], edge]
    return jnp.concatenate(pieces, axis=0)


def as_column(line):
    n = line.shape[1]
    square = lax.broadcasted_iota(jnp.int32, (n, n), 0) == lax.broadcasted_iota(
        jnp.int32, (n, n), 1
    )
    return jnp.sum(jnp.where(square, line.astype(F32), 0.0), axis=1, keepdims=True)


def kernel(
    dims,
    seg_hbm,
    w_hbm,
    gain_ref,
    head_ref,
    group_ref,
    pos_ref,
    full,
    proj_out,
    gain_out,
    seg_ref,
    w_ref,
    x3,
    conv,
    n_t,
    unit,
    dgelu,
    pooled,
    hgrad,
    g3,
    embeds,
    acc,
    work,
    r_a1,
    r_b1,
    r_a2,
    r_b2,
    r_z,
    pacc,
    pwork,
    pr_a1,
    pr_b1,
    pr_a2,
    pr_b2,
    pr_z,
    pfull,
    gc,
    gl,
    gh,
    gz,
    send_sem,
    recv_sem,
    load_sem,
):
    n_row, n_grp, n_hi, n_lo, n_z, total_segments = dims
    segs, length, chans = seg_ref.shape
    proj = head_ref.shape[1]
    n_taps = w_ref.shape[0]
    half = chans // 2
    quarter = chans // 4
    row = lax.axis_index("row")
    grp = lax.axis_index("grp")
    hi, lo = lax.div(row, n_lo), lax.rem(row, n_lo)
    z, core = lax.div(grp, 2), lax.rem(grp, 2)
    links = Links(send_sem, recv_sem)

    sibling = (row, z * 2 + (1 - core))
    row_peers = [(lax.rem(row + j, n_row), grp) for j in range(1, n_row)]
    lo_peers = [(lax.rem(lo + j, n_lo)) for j in range(1, n_lo)]
    hi_peers = [(lax.rem(hi + j, n_hi)) for j in range(1, n_hi)]
    z_peers = [(lax.rem(z + j, n_z)) for j in range(1, n_z)]

    def lo_dev(p):
        return (hi * n_lo + p, grp)

    def hi_dev(p):
        return (p * n_lo + lo, grp)

    def z_dev(p):
        return (row, p * 2 + core)

    barrier = pltpu.get_barrier_semaphore()
    everyone = [sibling] + row_peers + [z_dev(p) for p in z_peers]
    for device in everyone:
        pl.semaphore_signal(barrier, inc=1, device_id=device, device_id_type=MESH)

    block = BLOCK_SEGS * length
    n_blocks = segs // BLOCK_SEGS

    def seg_load(b):
        part = pl.ds(b * BLOCK_SEGS, BLOCK_SEGS)
        return pltpu.make_async_copy(seg_hbm.at[part], seg_ref.at[part], load_sem.at[b])

    w_loads = [
        pltpu.make_async_copy(w_hbm.at[k], w_ref.at[k], load_sem.at[n_blocks + k])
        for k in range(n_taps)
    ]
    seg_load(0).start()
    for load in w_loads:
        load.start()
    for b in range(1, n_blocks):
        seg_load(b).start()
    group_one = as_column(group_ref[...]).astype(jnp.int32)
    hot = jnp.where(
        group_one == lax.broadcasted_iota(jnp.int32, (segs, proj), 1), 1.0, 0.0
    ).astype(F32)
    embeds[row, :, proj:] = hot

    def norm_block(b):
        seg_load(b).wait()
        for i in range(BLOCK_SEGS):
            s = b * BLOCK_SEGS + i
            inputs = seg_ref[s].astype(F32)
            scale = lax.rsqrt(jnp.mean(inputs * inputs, axis=-1, keepdims=True) + EPS)
            normal = inputs * scale
            unit[s] = normal
            normed = normal * gain_ref[...]
            rows = slice(i * length, (i + 1) * length)
            x3[b % 2, rows, 0:chans] = shift_rows(normed, DILATION_GAP, length).astype(BF16)
            x3[b % 2, rows, chans : 2 * chans] = normed.astype(BF16)
            x3[b % 2, rows, 2 * chans : 3 * chans] = shift_rows(
                normed, -DILATION_GAP, length
            ).astype(BF16)
            n_t[s] = normed.T.astype(BF16)

    def conv_block(b):
        conv[b % 2] = jnp.dot(
            x3[b % 2], w_ref[...].reshape(n_taps * chans, chans), preferred_element_type=F32
        )

    def gelu_block(b):
        for i in range(BLOCK_SEGS):
            s = b * BLOCK_SEGS + i
            total = jnp.zeros((8, chans), F32)
            step = 16
            for q in range(length // step):
                rows = slice(i * length + q * step, i * length + (q + 1) * step)
                v = conv[b % 2, rows, :]
                v2 = v * v
                th = jnp.tanh(v * (GELU_A + (GELU_A * GELU_B) * v2))
                cdf = 0.5 + 0.5 * th
                hidden = seg_ref[s, q * step : (q + 1) * step].astype(F32) + v * cdf
                slope = (0.5 * GELU_A) + (1.5 * GELU_A * GELU_B) * v2
                dgelu[s, q * step : (q + 1) * step] = cdf + v * (1.0 - th * th) * slope
                total = total + hidden.reshape(step // 8, 8, chans).sum(axis=0)
            pooled[s : s + 1, :] = jnp.sum(total, axis=0, keepdims=True) * (1.0 / length)

    for phase in range(n_blocks + 2):
        if phase == 1:
            for load in w_loads:
                load.wait()
        if 1 <= phase <= n_blocks:
            conv_block(phase - 1)
        if phase < n_blocks:
            norm_block(phase)
        if phase >= 2:
            gelu_block(phase - 2)

    pool16 = pooled[...].astype(BF16)
    projected = jnp.dot(pool16, head_ref[...], preferred_element_type=F32)
    inv = lax.rsqrt(jnp.mean(projected * projected, axis=-1, keepdims=True) + EPS)
    embed = projected * inv * proj ** (-0.5)
    embeds[row, :, 0:proj] = embed
    pl.semaphore_wait(barrier, len(everyone))
    moves = [links.send(embeds.at[row], embeds.at[row], device) for device in row_peers]
    for move in moves:
        move.wait_recv()
    every = embeds[...].reshape(n_row * segs, 2 * proj)
    e_all, hot_all = every[:, :proj], every[:, proj:]
    count = n_row * segs
    contract = (((1,), (1,)), ((), ()))

    def scores_of(left):
        return (
            lax.dot_general(left, e_all, contract, precision=HIGHEST, preferred_element_type=F32)
            / LOGIT_DIVISOR
        )

    def same_of(left, first):
        match = lax.dot_general(left, hot_all, contract, preferred_element_type=F32)
        shape = match.shape
        own = first + lax.broadcasted_iota(jnp.int32, shape, 0)
        return jnp.where(own != lax.broadcasted_iota(jnp.int32, shape, 1), match, 0.0)

    s_full, m_full = scores_of(e_all), same_of(hot_all, 0)
    log_row = jnp.log(
        jnp.sum(jnp.where(m_full > 0.5, jnp.exp(s_full), 0.0), axis=0, keepdims=True)
    )
    s_own, m_own = scores_of(embed), same_of(hot, row * segs) > 0.5
    log_own = jnp.log(jnp.sum(jnp.where(m_own, jnp.exp(s_own), 0.0), axis=1, keepdims=True))
    mix = jnp.where(m_own, jnp.exp(s_own - log_own) + jnp.exp(s_own - log_row), 0.0)
    mix = mix - jnp.where(
        as_column(pos_ref[...]).astype(jnp.int32)
        == lax.broadcasted_iota(jnp.int32, (segs, count), 1),
        2.0,
        0.0,
    )
    embed_grad = (total_segments ** (-0.5) / LOGIT_DIVISOR) * jnp.dot(
        mix, e_all, precision=HIGHEST, preferred_element_type=F32
    )
    inner = jnp.mean(embed_grad * projected, axis=-1, keepdims=True)
    projected_grad = proj ** (-0.5) * (embed_grad * inv - projected * (inv * inv * inv * inner))
    hgrad[...] = (
        lax.dot_general(
            projected_grad,
            head_ref[...].astype(F32),
            contract,
            precision=HIGHEST,
            preferred_element_type=F32,
        )
        / length
    )

    def tiles(values, like):
        need = math.prod(like[:-1])
        if need > values.shape[0]:
            pad = jnp.zeros((need - values.shape[0], values.shape[1]), F32)
            values = jnp.concatenate([values, pad], axis=0)
        return values.reshape(like)

    class Chunk:
        def __init__(self, fill, finish, buffers):
            self.fill, self.finish = fill, finish
            self.acc, self.w, self.ra1, self.rb1, self.ra2, self.rb2, self.rz, self.out = buffers
            self.moves = []

        def arrive(self):
            for move in self.moves:
                move.wait_recv()
            self.moves = []

        def go(self, src, dst, device):
            self.moves.append(links.send(src, dst, device))

        def stage0(self):
            self.fill(self.acc, 1 - core)
            self.go(self.acc.at[1 - core], self.w, sibling)
            self.fill(self.acc, core)

        def stage1(self):
            self.arrive()
            w = self.w
            w[...] = w[...] + self.acc[core]
            for j, p in enumerate(lo_peers):
                self.go(w.at[0, :, p], self.ra1.at[j], lo_dev(p))
            for j, p in enumerate(hi_peers):
                self.go(w.at[1, p], self.rb1.at[j], hi_dev(p))

        def stage2(self):
            self.arrive()
            w = self.w
            a = w[0, :, lo]
            for j in range(n_lo - 1):
                a = a + self.ra1[j]
            w[0, :, lo] = a
            b = w[1, hi]
            for j in range(n_hi - 1):
                b = b + self.rb1[j]
            w[1, hi] = b
            for j, p in enumerate(hi_peers):
                self.go(w.at[0, p, lo], self.ra2.at[j], hi_dev(p))
            for j, p in enumerate(lo_peers):
                self.go(w.at[1, hi, p], self.rb2.at[j], lo_dev(p))

        def stage3(self):
            self.arrive()
            w = self.w
            a = w[0, hi, lo]
            for j in range(n_hi - 1):
                a = a + self.ra2[j]
            w[0, hi, lo] = a
            b = w[1, hi, lo]
            for j in range(n_lo - 1):
                b = b + self.rb2[j]
            w[1, hi, lo] = b
            for j, p in enumerate(z_peers):
                self.go(w.at[:, hi, lo, p], self.rz.at[j], z_dev(p))

        def stage4(self):
            self.arrive()
            total = self.w[:, hi, lo, z]
            for j in range(n_z - 1):
                total = total + self.rz[j]
            self.out[core, :, hi, lo, z] = total
            place = self.out.at[core, :, hi, lo, z]
            for p in z_peers:
                self.go(place, place, z_dev(p))

        def stage5(self):
            self.arrive()
            place = self.out.at[core, 0, hi, lo]
            for p in hi_peers:
                self.go(place, place, hi_dev(p))
            place = self.out.at[core, 1, hi, lo]
            for p in lo_peers:
                self.go(place, place, lo_dev(p))

        def stage6(self):
            self.arrive()
            place = self.out.at[core, 0, :, lo]
            for p in lo_peers:
                self.go(place, place, lo_dev(p))
            place = self.out.at[core, 1, hi]
            for p in hi_peers:
                self.go(place, place, hi_dev(p))

        def stage7(self):
            self.arrive()
            place = self.out.at[core]
            self.go(place, place, sibling)

        def stage8(self):
            self.arrive()
            self.finish()

    def put(acc_, side, values):
        for part in range(2):
            acc_[side, part] = tiles(
                values[:, part * quarter : (part + 1) * quarter], acc_.shape[2:]
            )

    parts = acc.shape[0] // n_taps
    part_rows = chans // parts

    def fill_tap(c, acc_, side):
        k, part = c // parts, c % parts
        first = part * part_rows
        lhs = jnp.concatenate([n_t[s, first : first + part_rows] for s in range(segs)], axis=1)
        put(acc_, side, jnp.dot(lhs, g3[k, side], preferred_element_type=F32))

    def store_proj():
        for side in range(2):
            for part in range(2):
                first = side * half + part * quarter
                block_t = pfull[side, part].reshape(-1, quarter)[:proj]
                proj_out[first : first + quarter, :] = block_t.T

    pool32 = pool16.astype(F32)
    proj_t = lax.dot_general(
        projected_grad,
        pool32,
        (((0,), (0,)), ((), ())),
        precision=HIGHEST,
        preferred_element_type=F32,
    )
    for side in range(2):
        put(pacc, side, proj_t[:, side * half : (side + 1) * half])

    proj_buffers = (pacc, pwork, pr_a1, pr_b1, pr_a2, pr_b2, pr_z, pfull)
    tap_buffers = (acc, work, r_a1, r_b1, r_a2, r_b2, r_z, full)
    chunks = [Chunk(lambda acc_, side: None, store_proj, proj_buffers)]
    chunks += [
        Chunk(
            functools.partial(fill_tap, c),
            lambda: None,
            [buffer.at[c] for buffer in tap_buffers],
        )
        for c in sorted(range(n_taps * parts), key=lambda c: c // parts != n_taps // 2)
    ]
    chunks[0].stage0()

    middle = n_taps // 2

    @pl.loop(0, segs)
    def _(s):
        grad = (dgelu[s] * hgrad[pl.ds(s, 1), :]).astype(BF16)
        rows = pl.ds(pl.multiple_of(s * length, length), length)
        for side in range(2):
            g3[middle, side, rows, :] = grad[:, side * half : (side + 1) * half]

    def shift_grads():
        @pl.loop(0, segs)
        def _(s):
            rows = pl.ds(pl.multiple_of(s * length, length), length)
            for side in range(2):
                grad = g3[middle, side, rows, :].astype(F32)
                for k in range(n_taps):
                    if k != middle:
                        by = (k - middle) * DILATION_GAP
                        g3[k, side, rows, :] = shift_rows(grad, by, length).astype(BF16)

    gain_state = {"sum": jnp.zeros((8, chans), F32), "moves": []}
    n_pieces = segs // BLOCK_SEGS

    def gain_piece(p):
        rows = slice(p * block, (p + 1) * block)
        lhs = jnp.concatenate(
            [g3[k, side, rows, :] for k in range(n_taps) for side in range(2)], axis=1
        )
        rhs = jnp.concatenate([w_ref[k] for k in range(n_taps)], axis=1)
        back = lax.dot_general(lhs, rhs, contract, preferred_element_type=F32)
        term = back * unit[p * BLOCK_SEGS : (p + 1) * BLOCK_SEGS].reshape(block, chans)
        gain_state["sum"] = gain_state["sum"] + term.reshape(block // 8, 8, chans).sum(axis=0)

    def gain_hop(buffer, index, devices):
        for move in gain_state["moves"]:
            move.wait_recv()
        buffer[index] = gain_state["sum"]
        gain_state["moves"] = [
            links.send(buffer.at[index], buffer.at[index], device) for device in devices
        ]
        gain_state["buffer"] = buffer

    def gain_sum():
        for move in gain_state["moves"]:
            move.wait_recv()
        gain_state["moves"] = []
        buffer = gain_state["buffer"]
        total = buffer[0]
        for j in range(1, buffer.shape[0]):
            total = total + buffer[j]
        gain_state["sum"] = total

    def gain_first():
        gain_state["sum"] = jnp.broadcast_to(
            jnp.sum(gain_state["sum"], axis=0, keepdims=True), (8, chans)
        )
        gain_hop(gc, core, [sibling])

    def gain_lo():
        gain_sum()
        gain_hop(gl, lo, [lo_dev(p) for p in lo_peers])

    def gain_hi():
        gain_sum()
        gain_hop(gh, hi, [hi_dev(p) for p in hi_peers])

    def gain_z():
        gain_sum()
        gain_hop(gz, z, [z_dev(p) for p in z_peers])

    def gain_end():
        gain_sum()
        gain_out[...] = gain_state["sum"][:1]

    extras = [functools.partial(gain_piece, p) for p in range(n_pieces)]
    extras += [gain_first, gain_lo, gain_hi, gain_z, gain_end]

    n_stages = 9
    for step in range(n_stages + len(chunks) - 1):
        for c, chunk in enumerate(chunks):
            stage = step - c
            if 0 <= stage < n_stages and (step > 0 or c > 0):
                getattr(chunk, "stage" + str(stage))()
        if step == parts:
            shift_grads()
        if step >= 3 and extras:
            extras.pop(0)()
    while extras:
        extras.pop(0)()
    for copy in links.copies:
        copy.wait_send()


def place_kernel(full, projector, gains, taps_out, projector_out, gains_out, sems):
    pairs = [(projector, projector_out), (gains, gains_out)]
    n_chunks, _, _, n_hi, n_lo, n_z, t, _, quarter = full.shape
    for c in range(n_chunks):
        for side in range(2):
            for part in range(2):
                first = (2 * side + part) * quarter
                dst = taps_out.at[c, :, :, :, :, :, pl.ds(first, quarter)]
                pairs.append((full.at[c, side, part], dst))
    copies = [pltpu.make_async_copy(*pair, sems.at[i]) for i, pair in enumerate(pairs)]
    for copy in copies:
        copy.start()
    for copy in copies:
        copy.wait()


def body(mesh_sizes, segments, conv_weight, gain, head, group, positive):
    n_row, n_grp = mesh_sizes
    n_lo = 2
    n_hi, n_z = n_row // n_lo, n_grp // 2
    shards = n_hi * n_lo * n_z
    records = segments[0]
    segs, length, chans = records.shape
    n_taps = conv_weight.shape[0]
    proj = head.shape[1]
    half, quarter = chans // 2, chans // 4
    count = n_row * segs
    parts = max(1, min(PARTS, chans // (8 * shards)))
    n_chunks = n_taps * parts
    t = -(-chans // (8 * shards * parts))
    tp = -(-proj // (8 * shards))

    def chunk_shapes(t, lead):
        grid = (n_hi, n_lo, n_z, t, 8)
        return [
            pltpu.VMEM(lead + (2, 2) + grid + (quarter,), F32),
            pltpu.VMEM(lead + (2,) + grid + (quarter,), F32),
            pltpu.VMEM(lead + (n_lo - 1, n_hi, n_z, t, 8, quarter), F32),
            pltpu.VMEM(lead + (n_hi - 1, n_lo, n_z, t, 8, quarter), F32),
            pltpu.VMEM(lead + (n_hi - 1, n_z, t, 8, quarter), F32),
            pltpu.VMEM(lead + (n_lo - 1, n_z, t, 8, quarter), F32),
            pltpu.VMEM(lead + (n_z - 1, 2, t, 8, quarter), F32),
            pltpu.VMEM(lead + (2, 2) + grid + (quarter,), F32),
        ]

    peers = (n_lo - 1) + (n_hi - 1)
    copies = (n_chunks + 1) * 2 * (1 + 2 * peers + n_z - 1)
    copies += (n_row - 1) + 1 + peers + n_z - 1
    rows = segs * length
    scratch = [
        pltpu.VMEM(records.shape, BF16),
        pltpu.VMEM(conv_weight.shape, BF16),
        pltpu.VMEM((2, BLOCK_SEGS * length, n_taps * chans), BF16),
        pltpu.VMEM((2, BLOCK_SEGS * length, chans), F32),
        pltpu.VMEM((segs, chans, length), BF16),
        pltpu.VMEM((segs, length, chans), F32),
        pltpu.VMEM((segs, length, chans), F32),
        pltpu.VMEM((segs, chans), F32),
        pltpu.VMEM((segs, chans), F32),
        pltpu.VMEM((n_taps, 2, rows, half), BF16),
        pltpu.VMEM((n_row, segs, 2 * proj), F32),
        *chunk_shapes(t, (n_chunks,))[:-1],
        *chunk_shapes(tp, ()),
        pltpu.VMEM((2, 8, chans), F32),
        pltpu.VMEM((n_lo, 8, chans), F32),
        pltpu.VMEM((n_hi, 8, chans), F32),
        pltpu.VMEM((n_z, 8, chans), F32),
        pltpu.SemaphoreType.DMA((copies,)),
        pltpu.SemaphoreType.DMA((copies,)),
        pltpu.SemaphoreType.DMA((segs // BLOCK_SEGS + n_taps,)),
    ]
    vmem = pl.BlockSpec(memory_space=pltpu.VMEM)
    hbm = pl.BlockSpec(memory_space=pltpu.HBM)
    flops = 3 * 2 * rows * chans * chans * n_taps
    taps, projector, gains = pl.pallas_call(
        functools.partial(kernel, (n_row, n_grp, n_hi, n_lo, n_z, count * n_grp)),
        out_shape=(
            pltpu.VMEM((n_chunks, 2, 2, n_hi, n_lo, n_z, t, 8, quarter), F32),
            pltpu.VMEM((chans, proj), F32),
            pltpu.VMEM((1, chans), F32),
        ),
        in_specs=[hbm] * 2 + [vmem] * 4,
        out_specs=(vmem, vmem, vmem),
        scratch_shapes=scratch,
        compiler_params=pltpu.CompilerParams(
            collective_id=0, has_side_effects=True, vmem_limit_bytes=52 * 1024 * 1024
        ),
        cost_estimate=pl.CostEstimate(
            flops=flops, bytes_accessed=8 * 1024 * 1024, transcendentals=rows * chans
        ),
    )(records, conv_weight, gain[None, :], head, group, positive)
    taps, projector, gains = pl.pallas_call(
        place_kernel,
        out_shape=(
            jax.ShapeDtypeStruct((n_chunks, n_hi, n_lo, n_z, t, 8, chans), F32),
            jax.ShapeDtypeStruct((chans, proj), F32),
            jax.ShapeDtypeStruct((1, chans), F32),
        ),
        in_specs=[vmem] * 3,
        out_specs=(hbm,) * 3,
        scratch_shapes=[pltpu.SemaphoreType.DMA((4 * n_chunks + 2,))],
    )(taps, projector, gains)
    rows_each = chans // parts
    taps = taps.reshape(n_chunks, shards * t * 8, chans)[:, :rows_each]
    return taps.reshape(n_taps, chans, chans), gains.reshape(chans), projector


def solution(mesh):
    placed = (P("grp", "row", None, None), P(), P(), P(), P("grp", "row"), P("grp", "row"))
    return jax.shard_map(
        functools.partial(body, (mesh.shape["row"], mesh.shape["grp"])),
        mesh=mesh,
        in_specs=placed,
        out_specs=(P(), P(), P()),
        check_vma=False,
    )
```

```python
import functools
import math

import jax
import jax.numpy as jnp
from jax import lax
from jax.experimental import pallas as pl
from jax.experimental.pallas import tpu as pltpu
from jax.sharding import PartitionSpec as P

DILATION_GAP = 2
LOGIT_DIVISOR = 0.1
EPS = 1e-05
GELU_A = math.sqrt(2.0 / math.pi)
GELU_B = 0.044715
HIGHEST = lax.Precision.HIGHEST
MESH = pl.DeviceIdType.MESH
F32 = jnp.float32
BF16 = jnp.bfloat16
BLOCK_SEGS = 4
PARTS = 2
LAG = 0.55
EXTRA_FROM, EXTRA_EVERY = 14, 3


class Links:
    def __init__(self, send_sem, recv_sem):
        self.send_sem, self.recv_sem, self.count, self.copies = send_sem, recv_sem, 0, []

    def send(self, src, dst, device):
        copy = pltpu.make_async_remote_copy(
            src_ref=src,
            dst_ref=dst,
            send_sem=self.send_sem.at[self.count],
            recv_sem=self.recv_sem.at[self.count],
            device_id=device,
            device_id_type=MESH,
        )
        copy.start()
        self.count += 1
        self.copies.append(copy)
        return copy


def shift_rows(values, by, length):
    moved = pltpu.roll(values, by % length, 0)
    edge = moved[:8] if by > 0 else moved[length - 8 :]
    time = lax.broadcasted_iota(jnp.int32, edge.shape, 0)
    edge = jnp.where((time >= by) if by > 0 else (time < 8 + by), edge, 0.0)
    pieces = [edge, moved[8:]] if by > 0 else [moved[: length - 8], edge]
    return jnp.concatenate(pieces, axis=0)


def as_column(line):
    n = line.shape[1]
    square = lax.broadcasted_iota(jnp.int32, (n, n), 0) == lax.broadcasted_iota(
        jnp.int32, (n, n), 1
    )
    return jnp.sum(jnp.where(square, line.astype(F32), 0.0), axis=1, keepdims=True)


def kernel(
    dims,
    seg_hbm,
    w_hbm,
    gain_ref,
    head_ref,
    group_ref,
    pos_ref,
    full,
    proj_out,
    gain_out,
    seg_ref,
    w_ref,
    x3,
    conv,
    n_t,
    unit,
    dgelu,
    pooled,
    hgrad,
    g3,
    embeds,
    acc,
    work,
    r_a1,
    r_b1,
    r_a2,
    r_b2,
    r_z,
    pacc,
    pwork,
    pr_a1,
    pr_b1,
    pr_a2,
    pr_b2,
    pr_z,
    pfull,
    gc,
    gl,
    gh,
    gz,
    send_sem,
    recv_sem,
    load_sem,
):
    n_row, n_grp, n_hi, n_lo, n_z, total_segments = dims
    segs, length, chans = seg_ref.shape
    proj = head_ref.shape[1]
    n_taps = w_ref.shape[0]
    half = chans // 2
    quarter = chans // 4
    row = lax.axis_index("row")
    grp = lax.axis_index("grp")
    hi, lo = lax.div(row, n_lo), lax.rem(row, n_lo)
    z, core = lax.div(grp, 2), lax.rem(grp, 2)
    links = Links(send_sem, recv_sem)

    sibling = (row, z * 2 + (1 - core))
    row_peers = [(lax.rem(row + j, n_row), grp) for j in range(1, n_row)]
    lo_peers = [(lax.rem(lo + j, n_lo)) for j in range(1, n_lo)]
    hi_peers = [(lax.rem(hi + j, n_hi)) for j in range(1, n_hi)]
    z_peers = [(lax.rem(z + j, n_z)) for j in range(1, n_z)]

    def lo_dev(p):
        return (hi * n_lo + p, grp)

    def hi_dev(p):
        return (p * n_lo + lo, grp)

    def z_dev(p):
        return (row, p * 2 + core)

    barrier = pltpu.get_barrier_semaphore()
    everyone = [sibling] + row_peers + [z_dev(p) for p in z_peers]
    for device in everyone:
        pl.semaphore_signal(barrier, inc=1, device_id=device, device_id_type=MESH)

    block = BLOCK_SEGS * length
    n_blocks = segs // BLOCK_SEGS

    def seg_load(b):
        part = pl.ds(b * BLOCK_SEGS, BLOCK_SEGS)
        return pltpu.make_async_copy(seg_hbm.at[part], seg_ref.at[part], load_sem.at[b])

    w_loads = [
        pltpu.make_async_copy(w_hbm.at[k], w_ref.at[k], load_sem.at[n_blocks + k])
        for k in range(n_taps)
    ]
    seg_load(0).start()
    for load in w_loads:
        load.start()
    for b in range(1, n_blocks):
        seg_load(b).start()
    group_one = as_column(group_ref[...]).astype(jnp.int32)
    hot = jnp.where(
        group_one == lax.broadcasted_iota(jnp.int32, (segs, proj), 1), 1.0, 0.0
    ).astype(F32)
    embeds[row, :, proj:] = hot

    def norm_block(b):
        seg_load(b).wait()
        for i in range(BLOCK_SEGS):
            s = b * BLOCK_SEGS + i
            inputs = seg_ref[s].astype(F32)
            scale = lax.rsqrt(jnp.mean(inputs * inputs, axis=-1, keepdims=True) + EPS)
            normal = inputs * scale
            unit[s] = normal
            normed = normal * gain_ref[...]
            rows = slice(i * length, (i + 1) * length)
            x3[b % 2, rows, 0:chans] = shift_rows(normed, DILATION_GAP, length).astype(BF16)
            x3[b % 2, rows, chans : 2 * chans] = normed.astype(BF16)
            x3[b % 2, rows, 2 * chans : 3 * chans] = shift_rows(
                normed, -DILATION_GAP, length
            ).astype(BF16)
            n_t[s] = normed.T.astype(BF16)

    def conv_block(b):
        conv[b % 2] = jnp.dot(
            x3[b % 2], w_ref[...].reshape(n_taps * chans, chans), preferred_element_type=F32
        )

    def gelu_block(b):
        for i in range(BLOCK_SEGS):
            s = b * BLOCK_SEGS + i
            total = jnp.zeros((8, chans), F32)
            step = 16
            for q in range(length // step):
                rows = slice(i * length + q * step, i * length + (q + 1) * step)
                v = conv[b % 2, rows, :]
                v2 = v * v
                th = jnp.tanh(v * (GELU_A + (GELU_A * GELU_B) * v2))
                cdf = 0.5 + 0.5 * th
                hidden = seg_ref[s, q * step : (q + 1) * step].astype(F32) + v * cdf
                slope = (0.5 * GELU_A) + (1.5 * GELU_A * GELU_B) * v2
                dgelu[s, q * step : (q + 1) * step] = cdf + v * (1.0 - th * th) * slope
                total = total + hidden.reshape(step // 8, 8, chans).sum(axis=0)
            pooled[s : s + 1, :] = jnp.sum(total, axis=0, keepdims=True) * (1.0 / length)

    for phase in range(n_blocks + 2):
        if phase == 1:
            for load in w_loads:
                load.wait()
        if 1 <= phase <= n_blocks:
            conv_block(phase - 1)
        if phase < n_blocks:
            norm_block(phase)
        if phase >= 2:
            gelu_block(phase - 2)

    pool16 = pooled[...].astype(BF16)
    projected = jnp.dot(pool16, head_ref[...], preferred_element_type=F32)
    inv = lax.rsqrt(jnp.mean(projected * projected, axis=-1, keepdims=True) + EPS)
    embed = projected * inv * proj ** (-0.5)
    embeds[row, :, 0:proj] = embed
    pl.semaphore_wait(barrier, len(everyone))
    moves = [links.send(embeds.at[row], embeds.at[row], device) for device in row_peers]
    for move in moves:
        move.wait_recv()
    every = embeds[...].reshape(n_row * segs, 2 * proj)
    e_all, hot_all = every[:, :proj], every[:, proj:]
    count = n_row * segs
    contract = (((1,), (1,)), ((), ()))

    def scores_of(left):
        return (
            lax.dot_general(left, e_all, contract, precision=HIGHEST, preferred_element_type=F32)
            / LOGIT_DIVISOR
        )

    def same_of(left, first):
        match = lax.dot_general(left, hot_all, contract, preferred_element_type=F32)
        shape = match.shape
        own = first + lax.broadcasted_iota(jnp.int32, shape, 0)
        return jnp.where(own != lax.broadcasted_iota(jnp.int32, shape, 1), match, 0.0)

    s_full, m_full = scores_of(e_all), same_of(hot_all, 0)
    log_row = jnp.log(
        jnp.sum(jnp.where(m_full > 0.5, jnp.exp(s_full), 0.0), axis=0, keepdims=True)
    )
    s_own, m_own = scores_of(embed), same_of(hot, row * segs) > 0.5
    log_own = jnp.log(jnp.sum(jnp.where(m_own, jnp.exp(s_own), 0.0), axis=1, keepdims=True))
    mix = jnp.where(m_own, jnp.exp(s_own - log_own) + jnp.exp(s_own - log_row), 0.0)
    mix = mix - jnp.where(
        as_column(pos_ref[...]).astype(jnp.int32)
        == lax.broadcasted_iota(jnp.int32, (segs, count), 1),
        2.0,
        0.0,
    )
    embed_grad = (total_segments ** (-0.5) / LOGIT_DIVISOR) * jnp.dot(
        mix, e_all, precision=HIGHEST, preferred_element_type=F32
    )
    inner = jnp.mean(embed_grad * projected, axis=-1, keepdims=True)
    projected_grad = proj ** (-0.5) * (embed_grad * inv - projected * (inv * inv * inv * inner))
    hgrad[...] = (
        lax.dot_general(
            projected_grad,
            head_ref[...].astype(F32),
            contract,
            precision=HIGHEST,
            preferred_element_type=F32,
        )
        / length
    )

    def tiles(values, like):
        need = math.prod(like[:-1])
        if need > values.shape[0]:
            pad = jnp.zeros((need - values.shape[0], values.shape[1]), F32)
            values = jnp.concatenate([values, pad], axis=0)
        return values.reshape(like)

    class Chunk:
        def __init__(self, fill, finish, buffers):
            self.fill, self.finish = fill, finish
            self.acc, self.w, self.ra1, self.rb1, self.ra2, self.rb2, self.rz, self.out = buffers
            self.moves = []

        def arrive(self):
            for move in self.moves:
                move.wait_recv()
            self.moves = []

        def go(self, src, dst, device):
            self.moves.append(links.send(src, dst, device))

        def stage0(self):
            self.fill(self.acc, 1 - core)
            self.go(self.acc.at[1 - core], self.w, sibling)
            self.fill(self.acc, core)

        def stage1(self):
            self.arrive()
            w = self.w
            w[...] = w[...] + self.acc[core]
            for j, p in enumerate(lo_peers):
                self.go(w.at[0, :, p], self.ra1.at[j], lo_dev(p))
            for j, p in enumerate(hi_peers):
                self.go(w.at[1, p], self.rb1.at[j], hi_dev(p))

        def stage2(self):
            self.arrive()
            w = self.w
            a = w[0, :, lo]
            for j in range(n_lo - 1):
                a = a + self.ra1[j]
            w[0, :, lo] = a
            b = w[1, hi]
            for j in range(n_hi - 1):
                b = b + self.rb1[j]
            w[1, hi] = b
            for j, p in enumerate(hi_peers):
                self.go(w.at[0, p, lo], self.ra2.at[j], hi_dev(p))
            for j, p in enumerate(lo_peers):
                self.go(w.at[1, hi, p], self.rb2.at[j], lo_dev(p))

        def stage3(self):
            self.arrive()
            w = self.w
            a = w[0, hi, lo]
            for j in range(n_hi - 1):
                a = a + self.ra2[j]
            w[0, hi, lo] = a
            b = w[1, hi, lo]
            for j in range(n_lo - 1):
                b = b + self.rb2[j]
            w[1, hi, lo] = b
            for j, p in enumerate(z_peers):
                self.go(w.at[:, hi, lo, p], self.rz.at[j], z_dev(p))

        def stage4(self):
            self.arrive()
            total = self.w[:, hi, lo, z]
            for j in range(n_z - 1):
                total = total + self.rz[j]
            self.out[core, :, hi, lo, z] = total
            place = self.out.at[core, :, hi, lo, z]
            for p in z_peers:
                self.go(place, place, z_dev(p))

        def stage5(self):
            self.arrive()
            place = self.out.at[core, 0, hi, lo]
            for p in hi_peers:
                self.go(place, place, hi_dev(p))
            place = self.out.at[core, 1, hi, lo]
            for p in lo_peers:
                self.go(place, place, lo_dev(p))

        def stage6(self):
            self.arrive()
            place = self.out.at[core, 0, :, lo]
            for p in lo_peers:
                self.go(place, place, lo_dev(p))
            place = self.out.at[core, 1, hi]
            for p in hi_peers:
                self.go(place, place, hi_dev(p))

        def stage7(self):
            self.arrive()
            place = self.out.at[core]
            self.go(place, place, sibling)

        def stage8(self):
            self.arrive()
            self.finish()

    def put(acc_, side, values):
        for part in range(2):
            acc_[side, part] = tiles(
                values[:, part * quarter : (part + 1) * quarter], acc_.shape[2:]
            )

    parts = acc.shape[0] // n_taps
    part_rows = chans // parts

    shifted = []

    def fill_tap(c, acc_, side):
        k, part = c // parts, c % parts
        if k != n_taps // 2 and not shifted:
            shift_grads()
            shifted.append(True)
        first = part * part_rows
        lhs = jnp.concatenate([n_t[s, first : first + part_rows] for s in range(segs)], axis=1)
        put(acc_, side, jnp.dot(lhs, g3[k, side], preferred_element_type=F32))

    def store_proj():
        for side in range(2):
            for part in range(2):
                first = side * half + part * quarter
                block_t = pfull[side, part].reshape(-1, quarter)[:proj]
                proj_out[first : first + quarter, :] = block_t.T

    pool32 = pool16.astype(F32)
    proj_t = lax.dot_general(
        projected_grad,
        pool32,
        (((0,), (0,)), ((), ())),
        precision=HIGHEST,
        preferred_element_type=F32,
    )
    for side in range(2):
        put(pacc, side, proj_t[:, side * half : (side + 1) * half])

    proj_buffers = (pacc, pwork, pr_a1, pr_b1, pr_a2, pr_b2, pr_z, pfull)
    tap_buffers = (acc, work, r_a1, r_b1, r_a2, r_b2, r_z, full)
    chunks = [Chunk(lambda acc_, side: None, store_proj, proj_buffers)]
    chunks += [
        Chunk(
            functools.partial(fill_tap, c),
            lambda: None,
            [buffer.at[c] for buffer in tap_buffers],
        )
        for c in sorted(range(n_taps * parts), key=lambda c: c // parts != n_taps // 2)
    ]
    chunks[0].stage0()

    middle = n_taps // 2

    @pl.loop(0, segs)
    def _(s):
        grad = (dgelu[s] * hgrad[pl.ds(s, 1), :]).astype(BF16)
        rows = pl.ds(pl.multiple_of(s * length, length), length)
        for side in range(2):
            g3[middle, side, rows, :] = grad[:, side * half : (side + 1) * half]

    def shift_grads():
        @pl.loop(0, segs)
        def _(s):
            rows = pl.ds(pl.multiple_of(s * length, length), length)
            for side in range(2):
                grad = g3[middle, side, rows, :].astype(F32)
                for k in range(n_taps):
                    if k != middle:
                        by = (k - middle) * DILATION_GAP
                        g3[k, side, rows, :] = shift_rows(grad, by, length).astype(BF16)

    gain_state = {"sum": jnp.zeros((8, chans), F32), "moves": []}
    n_pieces = segs // BLOCK_SEGS

    def gain_piece(p):
        rows = slice(p * block, (p + 1) * block)
        lhs = jnp.concatenate(
            [g3[k, side, rows, :] for k in range(n_taps) for side in range(2)], axis=1
        )
        rhs = jnp.concatenate([w_ref[k] for k in range(n_taps)], axis=1)
        back = lax.dot_general(lhs, rhs, contract, preferred_element_type=F32)
        term = back * unit[p * BLOCK_SEGS : (p + 1) * BLOCK_SEGS].reshape(block, chans)
        gain_state["sum"] = gain_state["sum"] + term.reshape(block // 8, 8, chans).sum(axis=0)

    def gain_hop(buffer, index, devices):
        for move in gain_state["moves"]:
            move.wait_recv()
        buffer[index] = gain_state["sum"]
        gain_state["moves"] = [
            links.send(buffer.at[index], buffer.at[index], device) for device in devices
        ]
        gain_state["buffer"] = buffer

    def gain_sum():
        for move in gain_state["moves"]:
            move.wait_recv()
        gain_state["moves"] = []
        buffer = gain_state["buffer"]
        total = buffer[0]
        for j in range(1, buffer.shape[0]):
            total = total + buffer[j]
        gain_state["sum"] = total

    def gain_first():
        gain_state["sum"] = jnp.broadcast_to(
            jnp.sum(gain_state["sum"], axis=0, keepdims=True), (8, chans)
        )
        gain_hop(gc, core, [sibling])

    def gain_lo():
        gain_sum()
        gain_hop(gl, lo, [lo_dev(p) for p in lo_peers])

    def gain_hi():
        gain_sum()
        gain_hop(gh, hi, [hi_dev(p) for p in hi_peers])

    def gain_z():
        gain_sum()
        gain_hop(gz, z, [z_dev(p) for p in z_peers])

    def gain_end():
        gain_sum()
        gain_out[...] = gain_state["sum"][:1]

    extras = [functools.partial(gain_piece, p) for p in range(n_pieces)]
    extras += [gain_first, gain_lo, gain_hi, gain_z, gain_end]

    n_stages = 9
    order = sorted(
        (stage + LAG * c, c, stage) for c in range(len(chunks)) for stage in range(n_stages)
    )
    for i, (_, c, stage) in enumerate(order):
        if (c, stage) != (0, 0):
            getattr(chunks[c], "stage" + str(stage))()
        if i >= EXTRA_FROM and (i - EXTRA_FROM) % EXTRA_EVERY == 0 and extras:
            extras.pop(0)()
    while extras:
        extras.pop(0)()
    for copy in links.copies:
        copy.wait_send()


def place_kernel(full, projector, gains, taps_out, projector_out, gains_out, sems):
    pairs = [(projector, projector_out), (gains, gains_out)]
    n_chunks, _, _, n_hi, n_lo, n_z, t, _, quarter = full.shape
    for c in range(n_chunks):
        for side in range(2):
            for part in range(2):
                first = (2 * side + part) * quarter
                dst = taps_out.at[c, :, :, :, :, :, pl.ds(first, quarter)]
                pairs.append((full.at[c, side, part], dst))
    copies = [pltpu.make_async_copy(*pair, sems.at[i]) for i, pair in enumerate(pairs)]
    for copy in copies:
        copy.start()
    for copy in copies:
        copy.wait()


def body(mesh_sizes, segments, conv_weight, gain, head, group, positive):
    n_row, n_grp = mesh_sizes
    n_lo = 2
    n_hi, n_z = n_row // n_lo, n_grp // 2
    shards = n_hi * n_lo * n_z
    records = segments[0]
    segs, length, chans = records.shape
    n_taps = conv_weight.shape[0]
    proj = head.shape[1]
    half, quarter = chans // 2, chans // 4
    count = n_row * segs
    parts = max(1, min(PARTS, chans // (8 * shards)))
    n_chunks = n_taps * parts
    t = -(-chans // (8 * shards * parts))
    tp = -(-proj // (8 * shards))

    def chunk_shapes(t, lead):
        grid = (n_hi, n_lo, n_z, t, 8)
        return [
            pltpu.VMEM(lead + (2, 2) + grid + (quarter,), F32),
            pltpu.VMEM(lead + (2,) + grid + (quarter,), F32),
            pltpu.VMEM(lead + (n_lo - 1, n_hi, n_z, t, 8, quarter), F32),
            pltpu.VMEM(lead + (n_hi - 1, n_lo, n_z, t, 8, quarter), F32),
            pltpu.VMEM(lead + (n_hi - 1, n_z, t, 8, quarter), F32),
            pltpu.VMEM(lead + (n_lo - 1, n_z, t, 8, quarter), F32),
            pltpu.VMEM(lead + (n_z - 1, 2, t, 8, quarter), F32),
            pltpu.VMEM(lead + (2, 2) + grid + (quarter,), F32),
        ]

    peers = (n_lo - 1) + (n_hi - 1)
    copies = (n_chunks + 1) * 2 * (1 + 2 * peers + n_z - 1)
    copies += (n_row - 1) + 1 + peers + n_z - 1
    rows = segs * length
    scratch = [
        pltpu.VMEM(records.shape, BF16),
        pltpu.VMEM(conv_weight.shape, BF16),
        pltpu.VMEM((2, BLOCK_SEGS * length, n_taps * chans), BF16),
        pltpu.VMEM((2, BLOCK_SEGS * length, chans), F32),
        pltpu.VMEM((segs, chans, length), BF16),
        pltpu.VMEM((segs, length, chans), F32),
        pltpu.VMEM((segs, length, chans), F32),
        pltpu.VMEM((segs, chans), F32),
        pltpu.VMEM((segs, chans), F32),
        pltpu.VMEM((n_taps, 2, rows, half), BF16),
        pltpu.VMEM((n_row, segs, 2 * proj), F32),
        *chunk_shapes(t, (n_chunks,))[:-1],
        *chunk_shapes(tp, ()),
        pltpu.VMEM((2, 8, chans), F32),
        pltpu.VMEM((n_lo, 8, chans), F32),
        pltpu.VMEM((n_hi, 8, chans), F32),
        pltpu.VMEM((n_z, 8, chans), F32),
        pltpu.SemaphoreType.DMA((copies,)),
        pltpu.SemaphoreType.DMA((copies,)),
        pltpu.SemaphoreType.DMA((segs // BLOCK_SEGS + n_taps,)),
    ]
    vmem = pl.BlockSpec(memory_space=pltpu.VMEM)
    hbm = pl.BlockSpec(memory_space=pltpu.HBM)
    flops = 3 * 2 * rows * chans * chans * n_taps
    taps, projector, gains = pl.pallas_call(
        functools.partial(kernel, (n_row, n_grp, n_hi, n_lo, n_z, count * n_grp)),
        out_shape=(
            pltpu.VMEM((n_chunks, 2, 2, n_hi, n_lo, n_z, t, 8, quarter), F32),
            pltpu.VMEM((chans, proj), F32),
            pltpu.VMEM((1, chans), F32),
        ),
        in_specs=[hbm] * 2 + [vmem] * 4,
        out_specs=(vmem, vmem, vmem),
        scratch_shapes=scratch,
        compiler_params=pltpu.CompilerParams(
            collective_id=0, has_side_effects=True, vmem_limit_bytes=52 * 1024 * 1024
        ),
        cost_estimate=pl.CostEstimate(
            flops=flops, bytes_accessed=8 * 1024 * 1024, transcendentals=rows * chans
        ),
    )(records, conv_weight, gain[None, :], head, group, positive)
    taps, projector, gains = pl.pallas_call(
        place_kernel,
        out_shape=(
            jax.ShapeDtypeStruct((n_chunks, n_hi, n_lo, n_z, t, 8, chans), F32),
            jax.ShapeDtypeStruct((chans, proj), F32),
            jax.ShapeDtypeStruct((1, chans), F32),
        ),
        in_specs=[pl.BlockSpec(memory_space=pl.ANY)] * 3,
        out_specs=(hbm,) * 3,
        scratch_shapes=[pltpu.SemaphoreType.DMA((4 * n_chunks + 2,))],
        compiler_params=pltpu.CompilerParams(vmem_limit_bytes=2 * 1024 * 1024),
    )(taps, projector, gains)
    rows_each = chans // parts
    taps = taps.reshape(n_chunks, shards * t * 8, chans)[:, :rows_each]
    return taps.reshape(n_taps, chans, chans), gains.reshape(chans), projector


def solution(mesh):
    placed = (P("grp", "row", None, None), P(), P(), P(), P("grp", "row"), P("grp", "row"))
    return jax.shard_map(
        functools.partial(body, (mesh.shape["row"], mesh.shape["grp"])),
        mesh=mesh,
        in_specs=placed,
        out_specs=(P(), P(), P()),
        check_vma=False,
    )
```

```python
import functools
import math

import jax
import jax.numpy as jnp
from jax import lax
from jax.experimental import pallas as pl
from jax.experimental.pallas import tpu as pltpu
from jax.sharding import PartitionSpec as P

DILATION_GAP = 2
LOGIT_DIVISOR = 0.1
EPS = 1e-05
GELU_A = math.sqrt(2.0 / math.pi)
GELU_B = 0.044715
HIGHEST = lax.Precision.HIGHEST
MESH = pl.DeviceIdType.MESH
F32 = jnp.float32
BF16 = jnp.bfloat16
BLOCK_SEGS = 4
PARTS = 2
LAG = 0.6
EXTRA_FROM, EXTRA_EVERY = 14, 3


class Links:
    def __init__(self, send_sem, recv_sem):
        self.send_sem, self.recv_sem, self.count, self.copies = send_sem, recv_sem, 0, []

    def send(self, src, dst, device):
        copy = pltpu.make_async_remote_copy(
            src_ref=src,
            dst_ref=dst,
            send_sem=self.send_sem.at[self.count],
            recv_sem=self.recv_sem.at[self.count],
            device_id=device,
            device_id_type=MESH,
        )
        copy.start()
        self.count += 1
        self.copies.append(copy)
        return copy


def shift_rows(values, by, length):
    moved = pltpu.roll(values, by % length, 0)
    edge = moved[:8] if by > 0 else moved[length - 8 :]
    time = lax.broadcasted_iota(jnp.int32, edge.shape, 0)
    edge = jnp.where((time >= by) if by > 0 else (time < 8 + by), edge, 0.0)
    pieces = [edge, moved[8:]] if by > 0 else [moved[: length - 8], edge]
    return jnp.concatenate(pieces, axis=0)


def as_column(line):
    n = line.shape[1]
    square = lax.broadcasted_iota(jnp.int32, (n, n), 0) == lax.broadcasted_iota(
        jnp.int32, (n, n), 1
    )
    return jnp.sum(jnp.where(square, line.astype(F32), 0.0), axis=1, keepdims=True)


def kernel(
    dims,
    seg_hbm,
    w_hbm,
    gain_ref,
    head_ref,
    group_ref,
    pos_ref,
    full,
    proj_out,
    gain_out,
    seg_ref,
    w_ref,
    x3,
    conv,
    n_t,
    unit,
    dgelu,
    pooled,
    hgrad,
    g3,
    embeds,
    acc,
    work,
    r_a1,
    r_b1,
    r_a2,
    r_b2,
    r_z,
    pacc,
    pwork,
    pr_a1,
    pr_b1,
    pr_a2,
    pr_b2,
    pr_z,
    pfull,
    gc,
    gl,
    gh,
    gz,
    send_sem,
    recv_sem,
    load_sem,
):
    n_row, n_grp, n_hi, n_lo, n_z, total_segments = dims
    segs, length, chans = seg_ref.shape
    proj = head_ref.shape[1]
    n_taps = w_ref.shape[0]
    half = chans // 2
    quarter = chans // 4
    row = lax.axis_index("row")
    grp = lax.axis_index("grp")
    hi, lo = lax.div(row, n_lo), lax.rem(row, n_lo)
    z, core = lax.div(grp, 2), lax.rem(grp, 2)
    links = Links(send_sem, recv_sem)

    sibling = (row, z * 2 + (1 - core))
    row_peers = [(lax.rem(row + j, n_row), grp) for j in range(1, n_row)]
    lo_peers = [(lax.rem(lo + j, n_lo)) for j in range(1, n_lo)]
    hi_peers = [(lax.rem(hi + j, n_hi)) for j in range(1, n_hi)]
    z_peers = [(lax.rem(z + j, n_z)) for j in range(1, n_z)]

    def lo_dev(p):
        return (hi * n_lo + p, grp)

    def hi_dev(p):
        return (p * n_lo + lo, grp)

    def z_dev(p):
        return (row, p * 2 + core)

    barrier = pltpu.get_barrier_semaphore()
    everyone = [sibling] + row_peers + [z_dev(p) for p in z_peers]
    for device in everyone:
        pl.semaphore_signal(barrier, inc=1, device_id=device, device_id_type=MESH)

    block = BLOCK_SEGS * length
    n_blocks = segs // BLOCK_SEGS

    def seg_load(b):
        part = pl.ds(b * BLOCK_SEGS, BLOCK_SEGS)
        return pltpu.make_async_copy(seg_hbm.at[part], seg_ref.at[part], load_sem.at[b])

    w_loads = [
        pltpu.make_async_copy(w_hbm.at[k], w_ref.at[k], load_sem.at[n_blocks + k])
        for k in range(n_taps)
    ]
    seg_load(0).start()
    for load in w_loads:
        load.start()
    for b in range(1, n_blocks):
        seg_load(b).start()
    group_one = as_column(group_ref[...]).astype(jnp.int32)
    hot = jnp.where(
        group_one == lax.broadcasted_iota(jnp.int32, (segs, proj), 1), 1.0, 0.0
    ).astype(F32)
    embeds[row, :, proj:] = hot

    def norm_block(b):
        seg_load(b).wait()
        for i in range(BLOCK_SEGS):
            s = b * BLOCK_SEGS + i
            inputs = seg_ref[s].astype(F32)
            scale = lax.rsqrt(jnp.mean(inputs * inputs, axis=-1, keepdims=True) + EPS)
            normal = inputs * scale
            unit[s] = normal
            normed = normal * gain_ref[...]
            rows = slice(i * length, (i + 1) * length)
            x3[b % 2, rows, 0:chans] = shift_rows(normed, DILATION_GAP, length).astype(BF16)
            x3[b % 2, rows, chans : 2 * chans] = normed.astype(BF16)
            x3[b % 2, rows, 2 * chans : 3 * chans] = shift_rows(
                normed, -DILATION_GAP, length
            ).astype(BF16)
            n_t[s] = normed.T.astype(BF16)

    def conv_block(b):
        conv[b % 2] = jnp.dot(
            x3[b % 2], w_ref[...].reshape(n_taps * chans, chans), preferred_element_type=F32
        )

    def gelu_block(b):
        for i in range(BLOCK_SEGS):
            s = b * BLOCK_SEGS + i
            total = jnp.zeros((8, chans), F32)
            step = 16
            for q in range(length // step):
                rows = slice(i * length + q * step, i * length + (q + 1) * step)
                v = conv[b % 2, rows, :]
                v2 = v * v
                th = jnp.tanh(v * (GELU_A + (GELU_A * GELU_B) * v2))
                cdf = 0.5 + 0.5 * th
                hidden = seg_ref[s, q * step : (q + 1) * step].astype(F32) + v * cdf
                slope = (0.5 * GELU_A) + (1.5 * GELU_A * GELU_B) * v2
                dgelu[s, q * step : (q + 1) * step] = cdf + v * (1.0 - th * th) * slope
                total = total + hidden.reshape(step // 8, 8, chans).sum(axis=0)
            pooled[s : s + 1, :] = jnp.sum(total, axis=0, keepdims=True) * (1.0 / length)

    for phase in range(n_blocks + 2):
        if phase == 1:
            for load in w_loads:
                load.wait()
        if 1 <= phase <= n_blocks:
            conv_block(phase - 1)
        if phase < n_blocks:
            norm_block(phase)
        if phase >= 2:
            gelu_block(phase - 2)

    pool16 = pooled[...].astype(BF16)
    projected = jnp.dot(pool16, head_ref[...], preferred_element_type=F32)
    inv = lax.rsqrt(jnp.mean(projected * projected, axis=-1, keepdims=True) + EPS)
    embed = projected * inv * proj ** (-0.5)
    embeds[row, :, 0:proj] = embed
    pl.semaphore_wait(barrier, len(everyone))
    moves = [links.send(embeds.at[row], embeds.at[row], device) for device in row_peers]
    for move in moves:
        move.wait_recv()
    every = embeds[...].reshape(n_row * segs, 2 * proj)
    e_all, hot_all = every[:, :proj], every[:, proj:]
    count = n_row * segs
    contract = (((1,), (1,)), ((), ()))

    def scores_of(left):
        return (
            lax.dot_general(left, e_all, contract, precision=HIGHEST, preferred_element_type=F32)
            / LOGIT_DIVISOR
        )

    def same_of(left, first):
        match = lax.dot_general(left, hot_all, contract, preferred_element_type=F32)
        shape = match.shape
        own = first + lax.broadcasted_iota(jnp.int32, shape, 0)
        return jnp.where(own != lax.broadcasted_iota(jnp.int32, shape, 1), match, 0.0)

    s_full, m_full = scores_of(e_all), same_of(hot_all, 0)
    log_row = jnp.log(
        jnp.sum(jnp.where(m_full > 0.5, jnp.exp(s_full), 0.0), axis=0, keepdims=True)
    )
    s_own, m_own = scores_of(embed), same_of(hot, row * segs) > 0.5
    log_own = jnp.log(jnp.sum(jnp.where(m_own, jnp.exp(s_own), 0.0), axis=1, keepdims=True))
    mix = jnp.where(m_own, jnp.exp(s_own - log_own) + jnp.exp(s_own - log_row), 0.0)
    mix = mix - jnp.where(
        as_column(pos_ref[...]).astype(jnp.int32)
        == lax.broadcasted_iota(jnp.int32, (segs, count), 1),
        2.0,
        0.0,
    )
    embed_grad = (total_segments ** (-0.5) / LOGIT_DIVISOR) * jnp.dot(
        mix, e_all, precision=HIGHEST, preferred_element_type=F32
    )
    inner = jnp.mean(embed_grad * projected, axis=-1, keepdims=True)
    projected_grad = proj ** (-0.5) * (embed_grad * inv - projected * (inv * inv * inv * inner))
    hgrad[...] = (
        lax.dot_general(
            projected_grad,
            head_ref[...].astype(F32),
            contract,
            precision=HIGHEST,
            preferred_element_type=F32,
        )
        / length
    )

    def tiles(values, like):
        need = math.prod(like[:-1])
        if need > values.shape[0]:
            pad = jnp.zeros((need - values.shape[0], values.shape[1]), F32)
            values = jnp.concatenate([values, pad], axis=0)
        return values.reshape(like)

    class Chunk:
        def __init__(self, fill, finish, buffers):
            self.fill, self.finish = fill, finish
            self.acc, self.w, self.ra1, self.rb1, self.ra2, self.rb2, self.rz, self.out = buffers
            self.moves = []

        def arrive(self):
            for move in self.moves:
                move.wait_recv()
            self.moves = []

        def go(self, src, dst, device):
            self.moves.append(links.send(src, dst, device))

        def stage0(self):
            self.fill(self.acc, 1 - core)
            self.go(self.acc.at[1 - core], self.w, sibling)
            self.fill(self.acc, core)

        def stage1(self):
            self.arrive()
            w = self.w
            w[...] = w[...] + self.acc[core]
            for j, p in enumerate(lo_peers):
                self.go(w.at[0, :, p], self.ra1.at[j], lo_dev(p))
            for j, p in enumerate(hi_peers):
                self.go(w.at[1, p], self.rb1.at[j], hi_dev(p))

        def stage2(self):
            self.arrive()
            w = self.w
            a = w[0, :, lo]
            for j in range(n_lo - 1):
                a = a + self.ra1[j]
            w[0, :, lo] = a
            b = w[1, hi]
            for j in range(n_hi - 1):
                b = b + self.rb1[j]
            w[1, hi] = b
            for j, p in enumerate(hi_peers):
                self.go(w.at[0, p, lo], self.ra2.at[j], hi_dev(p))
            for j, p in enumerate(lo_peers):
                self.go(w.at[1, hi, p], self.rb2.at[j], lo_dev(p))

        def stage3(self):
            self.arrive()
            w = self.w
            a = w[0, hi, lo]
            for j in range(n_hi - 1):
                a = a + self.ra2[j]
            w[0, hi, lo] = a
            b = w[1, hi, lo]
            for j in range(n_lo - 1):
                b = b + self.rb2[j]
            w[1, hi, lo] = b
            for j, p in enumerate(z_peers):
                self.go(w.at[:, hi, lo, p], self.rz.at[j], z_dev(p))

        def stage4(self):
            self.arrive()
            total = self.w[:, hi, lo, z]
            for j in range(n_z - 1):
                total = total + self.rz[j]
            self.out[core, :, hi, lo, z] = total
            place = self.out.at[core, :, hi, lo, z]
            for p in z_peers:
                self.go(place, place, z_dev(p))

        def stage5(self):
            self.arrive()
            place = self.out.at[core, 0, hi, lo]
            for p in hi_peers:
                self.go(place, place, hi_dev(p))
            place = self.out.at[core, 1, hi, lo]
            for p in lo_peers:
                self.go(place, place, lo_dev(p))

        def stage6(self):
            self.arrive()
            place = self.out.at[core, 0, :, lo]
            for p in lo_peers:
                self.go(place, place, lo_dev(p))
            place = self.out.at[core, 1, hi]
            for p in hi_peers:
                self.go(place, place, hi_dev(p))

        def stage7(self):
            self.arrive()
            place = self.out.at[core]
            self.go(place, place, sibling)

        def stage8(self):
            self.arrive()
            self.finish()

    def put(acc_, side, values):
        for part in range(2):
            acc_[side, part] = tiles(
                values[:, part * quarter : (part + 1) * quarter], acc_.shape[2:]
            )

    parts = acc.shape[0] // n_taps
    part_rows = chans // parts

    shifted = []

    def fill_tap(c, acc_, side):
        k, part = c // parts, c % parts
        if k != n_taps // 2 and not shifted:
            shift_grads()
            shifted.append(True)
        first = part * part_rows
        lhs = jnp.concatenate([n_t[s, first : first + part_rows] for s in range(segs)], axis=1)
        put(acc_, side, jnp.dot(lhs, g3[k, side], preferred_element_type=F32))

    def store_proj():
        for side in range(2):
            for part in range(2):
                first = side * half + part * quarter
                block_t = pfull[side, part].reshape(-1, quarter)[:proj]
                proj_out[first : first + quarter, :] = block_t.T

    filled = []

    def fill_proj(acc_, side):
        if filled:
            return
        filled.append(True)
        pool32 = pool16.astype(F32)
        proj_t = lax.dot_general(
            projected_grad,
            pool32,
            (((0,), (0,)), ((), ())),
            precision=HIGHEST,
            preferred_element_type=F32,
        )
        for side in range(2):
            put(pacc, side, proj_t[:, side * half : (side + 1) * half])

    proj_buffers = (pacc, pwork, pr_a1, pr_b1, pr_a2, pr_b2, pr_z, pfull)
    tap_buffers = (acc, work, r_a1, r_b1, r_a2, r_b2, r_z, full)
    chunks = [
        Chunk(
            functools.partial(fill_tap, c),
            lambda: None,
            [buffer.at[c] for buffer in tap_buffers],
        )
        for c in sorted(range(n_taps * parts), key=lambda c: c // parts != n_taps // 2)
    ]
    chunks.append(Chunk(fill_proj, store_proj, proj_buffers))

    middle = n_taps // 2

    @pl.loop(0, segs, unroll=4)
    def _(s):
        grad = (dgelu[s] * hgrad[pl.ds(s, 1), :]).astype(BF16)
        rows = pl.ds(pl.multiple_of(s * length, length), length)
        for side in range(2):
            g3[middle, side, rows, :] = grad[:, side * half : (side + 1) * half]

    def shift_grads():
        @pl.loop(0, segs, unroll=2)
        def _(s):
            rows = pl.ds(pl.multiple_of(s * length, length), length)
            for side in range(2):
                grad = g3[middle, side, rows, :].astype(F32)
                for k in range(n_taps):
                    if k != middle:
                        by = (k - middle) * DILATION_GAP
                        g3[k, side, rows, :] = shift_rows(grad, by, length).astype(BF16)

    gain_state = {"sum": jnp.zeros((8, chans), F32), "moves": []}
    n_pieces = segs // BLOCK_SEGS

    def gain_piece(p):
        rows = slice(p * block, (p + 1) * block)
        lhs = jnp.concatenate(
            [g3[k, side, rows, :] for k in range(n_taps) for side in range(2)], axis=1
        )
        rhs = jnp.concatenate([w_ref[k] for k in range(n_taps)], axis=1)
        back = lax.dot_general(lhs, rhs, contract, preferred_element_type=F32)
        term = back * unit[p * BLOCK_SEGS : (p + 1) * BLOCK_SEGS].reshape(block, chans)
        gain_state["sum"] = gain_state["sum"] + term.reshape(block // 8, 8, chans).sum(axis=0)

    def gain_hop(buffer, index, devices):
        for move in gain_state["moves"]:
            move.wait_recv()
        buffer[index] = gain_state["sum"]
        gain_state["moves"] = [
            links.send(buffer.at[index], buffer.at[index], device) for device in devices
        ]
        gain_state["buffer"] = buffer

    def gain_sum():
        for move in gain_state["moves"]:
            move.wait_recv()
        gain_state["moves"] = []
        buffer = gain_state["buffer"]
        total = buffer[0]
        for j in range(1, buffer.shape[0]):
            total = total + buffer[j]
        gain_state["sum"] = total

    def gain_first():
        gain_state["sum"] = jnp.broadcast_to(
            jnp.sum(gain_state["sum"], axis=0, keepdims=True), (8, chans)
        )
        gain_hop(gc, core, [sibling])

    def gain_lo():
        gain_sum()
        gain_hop(gl, lo, [lo_dev(p) for p in lo_peers])

    def gain_hi():
        gain_sum()
        gain_hop(gh, hi, [hi_dev(p) for p in hi_peers])

    def gain_z():
        gain_sum()
        gain_hop(gz, z, [z_dev(p) for p in z_peers])

    def gain_end():
        gain_sum()
        gain_out[...] = gain_state["sum"][:1]

    extras = [functools.partial(gain_piece, p) for p in range(n_pieces)]
    extras += [gain_first, gain_lo, gain_hi, gain_z, gain_end]

    n_stages = 9
    order = sorted(
        (stage + LAG * c, c, stage) for c in range(len(chunks)) for stage in range(n_stages)
    )
    for i, (_, c, stage) in enumerate(order):
        getattr(chunks[c], "stage" + str(stage))()
        if i >= EXTRA_FROM and (i - EXTRA_FROM) % EXTRA_EVERY == 0 and extras:
            extras.pop(0)()
    while extras:
        extras.pop(0)()
    for copy in links.copies:
        copy.wait_send()


def place_kernel(full, projector, gains, taps_out, projector_out, gains_out, sems):
    pairs = [(projector, projector_out), (gains, gains_out)]
    n_chunks, _, _, n_hi, n_lo, n_z, t, _, quarter = full.shape
    for c in range(n_chunks):
        for side in range(2):
            for part in range(2):
                first = (2 * side + part) * quarter
                dst = taps_out.at[c, :, :, :, :, :, pl.ds(first, quarter)]
                pairs.append((full.at[c, side, part], dst))
    copies = [pltpu.make_async_copy(*pair, sems.at[i]) for i, pair in enumerate(pairs)]
    for copy in copies:
        copy.start()
    for copy in copies:
        copy.wait()


def body(mesh_sizes, segments, conv_weight, gain, head, group, positive):
    n_row, n_grp = mesh_sizes
    n_lo = 2
    n_hi, n_z = n_row // n_lo, n_grp // 2
    shards = n_hi * n_lo * n_z
    records = segments[0]
    segs, length, chans = records.shape
    n_taps = conv_weight.shape[0]
    proj = head.shape[1]
    half, quarter = chans // 2, chans // 4
    count = n_row * segs
    parts = max(1, min(PARTS, chans // (8 * shards)))
    n_chunks = n_taps * parts
    t = -(-chans // (8 * shards * parts))
    tp = -(-proj // (8 * shards))

    def chunk_shapes(t, lead):
        grid = (n_hi, n_lo, n_z, t, 8)
        return [
            pltpu.VMEM(lead + (2, 2) + grid + (quarter,), F32),
            pltpu.VMEM(lead + (2,) + grid + (quarter,), F32),
            pltpu.VMEM(lead + (n_lo - 1, n_hi, n_z, t, 8, quarter), F32),
            pltpu.VMEM(lead + (n_hi - 1, n_lo, n_z, t, 8, quarter), F32),
            pltpu.VMEM(lead + (n_hi - 1, n_z, t, 8, quarter), F32),
            pltpu.VMEM(lead + (n_lo - 1, n_z, t, 8, quarter), F32),
            pltpu.VMEM(lead + (n_z - 1, 2, t, 8, quarter), F32),
            pltpu.VMEM(lead + (2, 2) + grid + (quarter,), F32),
        ]

    peers = (n_lo - 1) + (n_hi - 1)
    copies = (n_chunks + 1) * 2 * (1 + 2 * peers + n_z - 1)
    copies += (n_row - 1) + 1 + peers + n_z - 1
    rows = segs * length
    scratch = [
        pltpu.VMEM(records.shape, BF16),
        pltpu.VMEM(conv_weight.shape, BF16),
        pltpu.VMEM((2, BLOCK_SEGS * length, n_taps * chans), BF16),
        pltpu.VMEM((2, BLOCK_SEGS * length, chans), F32),
        pltpu.VMEM((segs, chans, length), BF16),
        pltpu.VMEM((segs, length, chans), F32),
        pltpu.VMEM((segs, length, chans), F32),
        pltpu.VMEM((segs, chans), F32),
        pltpu.VMEM((segs, chans), F32),
        pltpu.VMEM((n_taps, 2, rows, half), BF16),
        pltpu.VMEM((n_row, segs, 2 * proj), F32),
        *chunk_shapes(t, (n_chunks,))[:-1],
        *chunk_shapes(tp, ()),
        pltpu.VMEM((2, 8, chans), F32),
        pltpu.VMEM((n_lo, 8, chans), F32),
        pltpu.VMEM((n_hi, 8, chans), F32),
        pltpu.VMEM((n_z, 8, chans), F32),
        pltpu.SemaphoreType.DMA((copies,)),
        pltpu.SemaphoreType.DMA((copies,)),
        pltpu.SemaphoreType.DMA((segs // BLOCK_SEGS + n_taps,)),
    ]
    vmem = pl.BlockSpec(memory_space=pltpu.VMEM)
    hbm = pl.BlockSpec(memory_space=pltpu.HBM)
    flops = 3 * 2 * rows * chans * chans * n_taps
    taps, projector, gains = pl.pallas_call(
        functools.partial(kernel, (n_row, n_grp, n_hi, n_lo, n_z, count * n_grp)),
        out_shape=(
            pltpu.VMEM((n_chunks, 2, 2, n_hi, n_lo, n_z, t, 8, quarter), F32),
            pltpu.VMEM((chans, proj), F32),
            pltpu.VMEM((1, chans), F32),
        ),
        in_specs=[hbm] * 2 + [vmem] * 4,
        out_specs=(vmem, vmem, vmem),
        scratch_shapes=scratch,
        compiler_params=pltpu.CompilerParams(
            collective_id=0, has_side_effects=True, vmem_limit_bytes=52 * 1024 * 1024
        ),
        cost_estimate=pl.CostEstimate(
            flops=flops, bytes_accessed=8 * 1024 * 1024, transcendentals=rows * chans
        ),
    )(records, conv_weight, gain[None, :], head, group, positive)
    taps, projector, gains = pl.pallas_call(
        place_kernel,
        out_shape=(
            jax.ShapeDtypeStruct((n_chunks, n_hi, n_lo, n_z, t, 8, chans), F32),
            jax.ShapeDtypeStruct((chans, proj), F32),
            jax.ShapeDtypeStruct((1, chans), F32),
        ),
        in_specs=[pl.BlockSpec(memory_space=pl.ANY)] * 3,
        out_specs=(hbm,) * 3,
        scratch_shapes=[pltpu.SemaphoreType.DMA((4 * n_chunks + 2,))],
        compiler_params=pltpu.CompilerParams(vmem_limit_bytes=2 * 1024 * 1024),
    )(taps, projector, gains)
    rows_each = chans // parts
    taps = taps.reshape(n_chunks, shards * t * 8, chans)[:, :rows_each]
    return taps.reshape(n_taps, chans, chans), gains.reshape(chans), projector


def solution(mesh):
    placed = (P("grp", "row", None, None), P(), P(), P(), P("grp", "row"), P("grp", "row"))
    return jax.shard_map(
        functools.partial(body, (mesh.shape["row"], mesh.shape["grp"])),
        mesh=mesh,
        in_specs=placed,
        out_specs=(P(), P(), P()),
        check_vma=False,
    )
```
